128 devices in a mesh: cuts: 8 (over x, core), intra: 16 (over z, y).
Axes of the slice: x: 4, y: 4, z: 4, core: 2. Of those that a mesh axis runs over, the one named last changes fastest.
Arguments:
- partials: float32 [8, 16, 2, 256, 8192], P('cuts', 'intra'), may hold values from -5 to 5
- errors: float32 [8, 2, 256, 8192], P('cuts', None, None, 'intra'), may hold values from -6 to 6
- start_seed: int32 [2, 8192, 32], P(None, 'intra'), may hold values from 0 to 65520
Outputs:
- gradient: bfloat16 [2, 256, 8192], replicated
- new_error: float32 [8, 2, 256, 8192], P('cuts', None, None, 'intra')
The draws below stay inside these ranges and needn't reach their ends.
All inputs are finite; a program needn't handle non-finite values.
Results may differ from the reference program's by a relative error of at most 0.001.
Values may be sent and summed in bfloat16 or wider, within the bound.
A program may use at most 128 MiB of HBM per device.

```python
import jax
import jax.numpy as jnp
from jax import lax

D = 8192
RANK = 32
LAYERS = 2
ROWS = 256
N_CUTS = 8
N_INTRA = 16


def set_ends(entries, own_key, low, largest):
    place = [jax.random.randint(jax.random.fold_in(own_key, axis), (), 0, length) for axis, length in enumerate(entries.shape)]
    widest = entries.shape.index(max(entries.shape))
    beside = place[:widest] + [(place[widest] + 1) % entries.shape[widest]] + place[widest + 1:]
    return entries.at[tuple(place)].set(low).at[tuple(beside)].set(largest)


def spiked(entries, own_key, source, target, blocks, factor):
    def block_of(position):
        return (jnp.arange(entries.shape[position]) // (entries.shape[position] // blocks)).reshape((-1,) + (1,) * (entries.ndim - 1 - position))

    one_side = jax.random.permutation(own_key, blocks)[block_of(target)]
    second = (block_of(target) + blocks // 2) % blocks
    return jnp.where((block_of(source) == one_side) | (block_of(source) == second), factor * entries, entries)


def shard_levels(stream_key, shape, shards, smallest, high):
    gain, own = 1.0, jax.random.fold_in(stream_key, 6)
    for position, parts in shards:
        heights = jnp.exp(jax.random.uniform(jax.random.fold_in(own, position), (parts,), jnp.float32, smallest / len(shards), high / len(shards)))
        gain = gain * jnp.repeat(heights, shape[position] // parts).reshape([-1 if axis == position else 1 for axis in range(len(shape))])
    return gain


def centred(stream_key, shape, deviation, reach, cuts=(), kind=jnp.bfloat16):
    result = jax.random.normal(stream_key, shape, jnp.float32) * deviation
    if len(cuts) > 0:
        result = shard_levels(stream_key, shape, cuts, -0.22, 0.18) * result
    return jnp.clip(result, min=-reach, max=reach).astype(kind)


def gaussian_with(rng, dims, scale, limit, split, heavy, held_as=jnp.bfloat16):
    result = scale * jax.random.normal(rng, dims, jnp.float32)
    if split:
        result = result * shard_levels(rng, dims, split, -0.22, 0.18)
    return jnp.clip(spiked(result, jax.random.fold_in(rng, 3), *heavy), -limit, limit).astype(held_as)


def setup_inputs(seed: int = 0) -> dict:
    streams_of = jax.random.split(jax.random.key(seed), 4)
    return {
        "partials": gaussian_with(streams_of[0], (N_CUTS, N_INTRA, LAYERS, ROWS, D), 0.25, 5.0, ((0, 8), (1, 16)), (1, 4, 16, 2.0), jnp.float32),
        "errors": centred(streams_of[1], (N_CUTS, LAYERS, ROWS, D), 0.5, 6.0, ((0, 8), (3, 16)), jnp.float32),
        "start_seed": set_ends(jax.random.randint(streams_of[2], (LAYERS, D, RANK), 0, 65521), jax.random.fold_in(streams_of[2], 1), 0, 65520).astype(jnp.int32),
    }


def orthonormal(left_factor):
    finished = []
    for column in range(left_factor.shape[-1]):
        vector = left_factor[..., column]
        for earlier in finished:
            vector = vector - lax.optimization_barrier(jnp.sum(earlier * vector, axis=-1, keepdims=True)) * earlier
        length = jnp.sqrt(lax.optimization_barrier(jnp.sum(vector * vector, axis=-1, keepdims=True)) + 1e-06)
        finished.append(vector / length)
    return jnp.stack(finished, axis=-1)

def reference(partials, errors, start_seed):
    summed = lax.optimization_barrier(jnp.sum(partials, axis=1))
    merged = summed + errors
    groups, layers, rows, width = merged.shape
    pieces = N_INTRA
    shard = width // pieces
    blocks = merged.reshape(groups, layers, rows, pieces, shard)
    start = (start_seed.astype(jnp.float32) - 32760.0) * (1.0 / 18918.0)
    start = start.reshape(layers, pieces, shard, RANK)
    left = jnp.einsum('clrjd,ljdk->ljrk', blocks, start, precision=lax.Precision.HIGHEST)
    basis = orthonormal(left)
    right = jnp.einsum('clrjd,ljrk->ljdk', blocks, basis, precision=lax.Precision.HIGHEST) / N_CUTS
    approx = jnp.einsum('ljrk,ljdk->lrjd', basis, right, precision=lax.Precision.HIGHEST)
    approx = approx.reshape(layers, rows, width)
    gradient = approx.astype(jnp.bfloat16)
    new_error = merged - approx[None]
    return (gradient, new_error)
```

```python
import functools

import jax
import jax.numpy as jnp
from jax import lax
from jax.experimental import pallas as pl
from jax.experimental.pallas import tpu as pltpu
from jax.sharding import PartitionSpec as P

MESH = pl.DeviceIdType.MESH
HIGHEST = lax.Precision.HIGHEST
STEPS = 8
LIMIT = 32767.0


def quantize(values):
    top = jnp.abs(values)
    while top.ndim > 2:
        top = jnp.max(top, axis=0)
    top = jnp.maximum(jnp.max(top, axis=0, keepdims=True), 1e-30)
    coded = jnp.round(values * (LIMIT / top)).astype(jnp.int32).astype(jnp.int16)
    return coded, top * (1.0 / LIMIT)


def restore(coded, scale):
    return coded.astype(jnp.int32).astype(jnp.float32) * scale


def exchange(part, errors, start, merged, basis_q, basis_s, right_q, right_s,
             own, error_v, send1, recv1, send2, recv2, sscale, rscale,
             left, left_all, vectors, basis, right, right_all, reduced, right_full,
             load_sem, error_sem, ssem, rsem, cut_send, cut_recv, plane_send, plane_recv, local_sem):
    cut = lax.axis_index("cuts")
    member = lax.axis_index("intra")
    y, z = lax.rem(member, 4), lax.div(member, 4)

    def wrap(v):
        return lax.rem(v + 8, 4)

    ring = (
        {"plus": (cut, z * 4 + wrap(y + 1)), "minus": (cut, z * 4 + wrap(y - 1)), "pos": y},
        {"plus": (cut, wrap(z + 1) * 4 + y), "minus": (cut, wrap(z - 1) * 4 + y), "pos": z},
    )

    def cut_peer(o):
        return lax.rem(cut + o, 8)

    def plane_peer(o):
        return lax.rem(member + o, 16)

    def load(g, _):
        for l in range(2):
            pltpu.make_async_copy(
                part.at[l, :, pl.ds(pl.multiple_of(g * 128, 128), 128)],
                own.at[l, lax.div(g, 16), lax.rem(lax.div(g, 4), 4), lax.rem(g, 4)],
                load_sem.at[l]).start()
        return 0

    lax.fori_loop(0, 64, load, 0)
    error_copy = pltpu.make_async_copy(errors, error_v, error_sem)
    error_copy.start()

    barrier = pltpu.get_barrier_semaphore()
    for o in range(1, 8):
        pl.semaphore_signal(barrier, inc=1, device_id=(cut_peer(o), member), device_id_type=MESH)
    for o in range(1, 16):
        pl.semaphore_signal(barrier, inc=1, device_id=(cut, plane_peer(o)), device_id_type=MESH)
    pl.semaphore_wait(barrier, 22)
    error_copy.wait()

    sends = (send1, send2)
    recvs = (recv1, recv2)

    def copies(t, s, p, m):
        axis = ring[s if p == 0 else 1 - s]
        to = axis["plus"] if m in (0, 2, 4) else axis["minus"]
        data = pltpu.make_async_remote_copy(
            src_ref=sends[p].at[t, s, m], dst_ref=recvs[p].at[t, s, m],
            send_sem=ssem.at[t, s, p, m, 0], recv_sem=rsem.at[t, s, p, m, 0],
            device_id=to, device_id_type=MESH)
        scale = pltpu.make_async_remote_copy(
            src_ref=sscale.at[t, s, p, m], dst_ref=rscale.at[t, s, p, m],
            send_sem=ssem.at[t, s, p, m, 1], recv_sem=rsem.at[t, s, p, m, 1],
            device_id=to, device_id_type=MESH)
        return data, scale

    def rows_of(t, s, h):
        return pl.ds(pl.multiple_of(lax.rem(t, 4) * 64 + s * 32 + h * 16, 16), 16)

    def term(t, s, p, q, h):
        l, rows = lax.div(t, 4), rows_of(t, s, h)
        if p == 0:
            return own[l, :, q, :, rows, :] if s == 0 else own[l, q, :, :, rows, :]
        return own[l, q, y, :, rows, :] if s == 0 else own[l, z, q, :, rows, :]

    def send(t, s, p, m, values):
        coded, scale = quantize(values)
        sends[p][t, s, m] = coded
        sscale[t, s, p, m] = scale
        for copy in copies(t, s, p, m):
            copy.start()

    def receive(t, s, p, m):
        for copy in copies(t, s, p, m):
            copy.wait_recv()
        return restore(recvs[p][t, s, m], rscale[t, s, p, m])

    def first(t, s, p):
        pos = ring[s if p == 0 else 1 - s]["pos"]
        send(t, s, p, 0, term(t, s, p, wrap(pos + 2), 0))
        send(t, s, p, 1, term(t, s, p, wrap(pos + 2), 1))
        send(t, s, p, 2, term(t, s, p, wrap(pos + 1), 1))
        send(t, s, p, 3, term(t, s, p, wrap(pos - 1), 0))

    def second(t, s, p):
        pos = ring[s if p == 0 else 1 - s]["pos"]
        send(t, s, p, 4, term(t, s, p, wrap(pos + 1), 0) + receive(t, s, p, 0))
        send(t, s, p, 5, term(t, s, p, wrap(pos - 1), 1) + receive(t, s, p, 1))

    def total(t, s, p, h):
        pos = ring[s if p == 0 else 1 - s]["pos"]
        pair = (3, 4) if h == 0 else (2, 5)
        return term(t, s, p, pos, h) + receive(t, s, p, pair[0]) + receive(t, s, p, pair[1])

    def step(t, _):
        @pl.when(t < STEPS)
        def _():
            @pl.when(lax.rem(t, 4) == 0)
            def _():
                l = lax.div(t, 4)
                pltpu.make_async_copy(own.at[l], own.at[l], load_sem.at[l]).wait()

            for s in range(2):
                first(t, s, 0)

        @pl.when((t >= 1) & (t < STEPS + 1))
        def _():
            for s in range(2):
                second(t - 1, s, 0)

        @pl.when((t >= 2) & (t < STEPS + 2))
        def _():
            u = t - 2
            l = lax.div(u, 4)
            for s in range(2):
                for h in range(2):
                    summed = total(u, s, 0, h)
                    if s == 0:
                        own[l, :, y, :, rows_of(u, s, h), :] = summed
                    else:
                        own[l, z, :, :, rows_of(u, s, h), :] = summed
                first(u, s, 1)

        @pl.when((t >= 3) & (t < STEPS + 3))
        def _():
            for s in range(2):
                second(t - 3, s, 1)

        @pl.when(t >= 4)
        def _():
            u = t - 4
            l = lax.div(u, 4)
            for s in range(2):
                for h in range(2):
                    rows = rows_of(u, s, h)
                    summed = total(u, s, 1, h)
                    wide = jnp.concatenate([summed[i] for i in range(4)], axis=1)
                    merged[l, rows, :] = wide + error_v[l, rows, :]

        return 0

    lax.fori_loop(0, STEPS + 4, step, 0)

    def cut_copy(kind, o, src, dst):
        return pltpu.make_async_remote_copy(
            src_ref=src, dst_ref=dst, send_sem=cut_send.at[kind, o], recv_sem=cut_recv.at[kind, o],
            device_id=(cut_peer(o), member), device_id_type=MESH)

    for l in range(2):
        left[l] = lax.dot_general(start[l], merged[l], (((1,), (1,)), ((), ())),
                                  precision=HIGHEST, preferred_element_type=jnp.float32)
    lefts = [cut_copy(0, o, left, left_all.at[cut]) for o in range(1, 8)]
    for copy in lefts:
        copy.start()
    left_all[cut] = left[...]
    for copy in lefts:
        copy.wait()
    summed_left = left_all[0]
    for c in range(1, 8):
        summed_left = summed_left + left_all[c]
    vectors[...] = summed_left

    later = lax.broadcasted_iota(jnp.int32, (32, 1), 0)

    def column(k, _):
        for l in range(2):
            v = vectors[l, pl.ds(k, 1), :]
            block = vectors[l]
            size = jnp.sum(v * v, axis=1, keepdims=True) + 1e-6
            dots = jnp.sum(block * v, axis=1, keepdims=True)
            basis[l, pl.ds(k, 1), :] = v / jnp.sqrt(size)
            vectors[l] = block - jnp.where(later > k, dots / size, 0.0) * v
        return 0

    lax.fori_loop(0, 32, column, 0)

    core = lax.rem(cut, 2)

    def plane_copies(o, which):
        there = (cut, plane_peer(o))
        return (
            [pltpu.make_async_remote_copy(
                src_ref=ref.at[core, member], dst_ref=ref.at[core, member],
                send_sem=plane_send.at[n, o], recv_sem=plane_recv.at[n, o],
                device_id=there, device_id_type=MESH)
             for n, ref in enumerate((basis_q, basis_s, right_q, right_s)) if n in which])

    coded, scale = quantize(basis[core])
    basis_q[core, member] = coded
    basis_s[core, member] = scale
    for o in range(1, 16):
        for copy in plane_copies(o, (0, 1)):
            copy.start()

    for l in range(2):
        wide = jnp.dot(basis[l], merged[l], precision=HIGHEST, preferred_element_type=jnp.float32)
        for i in range(4):
            right[l * 4 + i] = wide[:, i * 128:(i + 1) * 128]
    rights = [cut_copy(1, o, right.at[cut_peer(o)], right_all.at[cut]) for o in range(1, 8)]
    for copy in rights:
        copy.start()
    right_all[cut] = right[cut]
    for copy in rights:
        copy.wait()
    summed_right = right_all[0]
    for c in range(1, 8):
        summed_right = summed_right + right_all[c]
    reduced[...] = summed_right * 0.125
    gathers = [cut_copy(2, o, reduced, right_full.at[cut]) for o in range(1, 8)]
    for copy in gathers:
        copy.start()
    right_full[cut] = reduced[...]
    for copy in gathers:
        copy.wait()

    coded, scale = quantize(jnp.concatenate([right_full[core * 4 + i] for i in range(4)], axis=1))
    right_q[core, member] = coded
    right_s[core, member] = scale
    for o in range(1, 16):
        for copy in plane_copies(o, (2, 3)):
            copy.start()
    for o in range(1, 16):
        for copy in plane_copies(o, (0, 1, 2, 3)):
            copy.wait()

    sibling = (cut + 1 - 2 * core, member)
    swaps = [pltpu.make_async_remote_copy(
        src_ref=ref.at[core], dst_ref=ref.at[core], send_sem=local_sem.at[0, n], recv_sem=local_sem.at[1, n],
        device_id=sibling, device_id_type=MESH) for n, ref in enumerate((basis_q, basis_s, right_q, right_s))]
    for copy in swaps:
        copy.start()
    for copy in swaps:
        copy.wait()

    def drained(t, _):
        for s in range(2):
            for p in range(2):
                for m in range(6):
                    for copy in copies(t, s, p, m):
                        copy.wait_send()
        return 0

    lax.fori_loop(0, STEPS, drained, 0)


def decompress(member_ref, basis_q, basis_s, right_q, right_s, merged, gradient, new_error):
    j = pl.program_id(0)
    for l in range(2):
        b = restore(basis_q[l, 0], basis_s[l, 0])
        r = restore(right_q[l, 0], right_s[l, 0])
        b_high, r_high = b.astype(jnp.bfloat16), r.astype(jnp.bfloat16)
        b_low = (b - b_high.astype(jnp.float32)).astype(jnp.bfloat16)
        r_low = (r - r_high.astype(jnp.float32)).astype(jnp.bfloat16)
        approx = lax.dot_general(
            jnp.concatenate([b_high, b_high, b_low], axis=0),
            jnp.concatenate([r_high, r_low, r_high], axis=0),
            (((0,), (0,)), ((), ())), preferred_element_type=jnp.float32)
        gradient[l] = approx.astype(jnp.bfloat16)

        @pl.when(j == member_ref[0])
        def _():
            new_error[l] = merged[l] - approx


def body(partials, errors, start_seed):
    f32, i16 = jnp.float32, jnp.int16
    start = jnp.swapaxes((start_seed.astype(f32) - 32760.0) * (1.0 / 18918.0), 1, 2)
    vmem = pl.BlockSpec(memory_space=pltpu.VMEM)
    hbm = pl.BlockSpec(memory_space=pl.ANY)
    dma = pltpu.SemaphoreType.DMA
    merged, basis_q, basis_s, right_q, right_s = pl.pallas_call(
        exchange,
        out_shape=(
            jax.ShapeDtypeStruct((2, 256, 512), f32),
            jax.ShapeDtypeStruct((2, 16, 32, 256), i16),
            jax.ShapeDtypeStruct((2, 16, 1, 256), f32),
            jax.ShapeDtypeStruct((2, 16, 32, 512), i16),
            jax.ShapeDtypeStruct((2, 16, 1, 512), f32),
        ),
        in_specs=[hbm, hbm, vmem],
        out_specs=(vmem,) * 5,
        scratch_shapes=[
            pltpu.VMEM((2, 4, 4, 4, 256, 128), f32),
            pltpu.VMEM((2, 256, 512), f32),
            pltpu.VMEM((STEPS, 2, 6, 4, 4, 16, 128), i16),
            pltpu.VMEM((STEPS, 2, 6, 4, 4, 16, 128), i16),
            pltpu.VMEM((STEPS, 2, 6, 4, 16, 128), i16),
            pltpu.VMEM((STEPS, 2, 6, 4, 16, 128), i16),
            pltpu.VMEM((STEPS, 2, 2, 6, 1, 128), f32),
            pltpu.VMEM((STEPS, 2, 2, 6, 1, 128), f32),
            pltpu.VMEM((2, 32, 256), f32),
            pltpu.VMEM((8, 2, 32, 256), f32),
            pltpu.VMEM((2, 32, 256), f32),
            pltpu.VMEM((2, 32, 256), f32),
            pltpu.VMEM((8, 32, 128), f32),
            pltpu.VMEM((8, 32, 128), f32),
            pltpu.VMEM((32, 128), f32),
            pltpu.VMEM((8, 32, 128), f32),
            dma((2,)),
            dma,
            dma((STEPS, 2, 2, 6, 2)),
            dma((STEPS, 2, 2, 6, 2)),
            dma((3, 8)),
            dma((3, 8)),
            dma((4, 16)),
            dma((4, 16)),
            dma((2, 4)),
        ],
        compiler_params=pltpu.CompilerParams(
            collective_id=0, has_side_effects=True, vmem_limit_bytes=56 * 1024 * 1024),
        name="exchange",
    )(partials.reshape(2, 256, 8192), errors.reshape(2, 256, 512), start)

    member = lax.axis_index("intra").astype(jnp.int32).reshape(1)
    gradient, new_error = pl.pallas_call(
        decompress,
        grid=(16,),
        out_shape=(
            jax.ShapeDtypeStruct((2, 256, 8192), jnp.bfloat16),
            jax.ShapeDtypeStruct((2, 256, 512), f32),
        ),
        in_specs=[
            pl.BlockSpec(memory_space=pltpu.SMEM),
            pl.BlockSpec((2, 1, 32, 256), lambda j: (0, j, 0, 0)),
            pl.BlockSpec((2, 1, 1, 256), lambda j: (0, j, 0, 0)),
            pl.BlockSpec((2, 1, 32, 512), lambda j: (0, j, 0, 0)),
            pl.BlockSpec((2, 1, 1, 512), lambda j: (0, j, 0, 0)),
            pl.BlockSpec((2, 256, 512), lambda j: (0, 0, 0)),
        ],
        out_specs=(
            pl.BlockSpec((2, 256, 512), lambda j: (0, 0, j)),
            pl.BlockSpec((2, 256, 512), lambda j: (0, 0, 0)),
        ),
        compiler_params=pltpu.CompilerParams(vmem_limit_bytes=32 * 1024 * 1024),
        name="decompress",
    )(member, basis_q, basis_s, right_q, right_s, merged)
    return gradient, new_error[None]


def solution(mesh):
    in_specs = (
        P("cuts", "intra", None, None, None),
        P("cuts", None, None, "intra"),
        P(None, "intra", None),
    )
    out_specs = (P(), P("cuts", None, None, "intra"))
    return jax.shard_map(body, mesh=mesh, in_specs=in_specs, out_specs=out_specs, check_vma=False)
```

```python
import functools

import jax
import jax.numpy as jnp
from jax import lax
from jax.experimental import pallas as pl
from jax.experimental.pallas import tpu as pltpu
from jax.sharding import PartitionSpec as P

MESH = pl.DeviceIdType.MESH
HIGHEST = lax.Precision.HIGHEST
STEPS = 8
LIMIT = 32767.0


def quantize(values):
    top = jnp.abs(values)
    while top.ndim > 2:
        top = jnp.max(top, axis=0)
    top = jnp.maximum(jnp.max(top, axis=0, keepdims=True), 1e-30)
    coded = jnp.round(values * (LIMIT / top)).astype(jnp.int32).astype(jnp.int16)
    return coded, top * (1.0 / LIMIT)


def restore(coded, scale):
    return coded.astype(jnp.int32).astype(jnp.float32) * scale


def exchange(part, errors, seed, merged_out, basis_q, basis_s, right_q, right_s,
             own, error_v, merged, start,
             sa1, sb1, sa2, sb2, ra1, rb1, ra2, rb2, ssa, ssb, rsa, rsb,
             left, left_all, basis, right, right_all, right_full,
             basis_send, right_send, scale_send,
             load_sem, error_sem, out_sem, send_sem, recv_sem, cut_send, cut_recv,
             plane_send, plane_recv, swap_sem):
    cut = lax.axis_index("cuts")
    member = lax.axis_index("intra")
    y, z = lax.rem(member, 4), lax.div(member, 4)
    core = lax.rem(cut, 2)

    def wrap(v):
        return lax.rem(v + 8, 4)

    ring = (
        {"plus": (cut, z * 4 + wrap(y + 1)), "minus": (cut, z * 4 + wrap(y - 1)), "pos": y},
        {"plus": (cut, wrap(z + 1) * 4 + y), "minus": (cut, wrap(z - 1) * 4 + y), "pos": z},
    )

    def cut_peer(o):
        return lax.rem(cut + o, 8)

    def plane_peer(o):
        return lax.rem(member + o, 16)

    def load(l, first, count, sem):
        rows = pl.ds(first, count)

        def group(g, _):
            pltpu.make_async_copy(
                part.at[l, rows, pl.ds(pl.multiple_of(g * 128, 128), 128)],
                own.at[l, lax.div(g, 16), lax.rem(lax.div(g, 4), 4), lax.rem(g, 4), rows],
                load_sem.at[sem]).start()
            return 0

        lax.fori_loop(0, 64, group, 0)

    def loaded(l, first, count, sem):
        there = own.at[l, :, :, :, pl.ds(first, count)]
        pltpu.make_async_copy(there, there, load_sem.at[sem]).wait()

    load(0, 0, 64, 0)

    barrier = pltpu.get_barrier_semaphore()
    for o in range(1, 8):
        pl.semaphore_signal(barrier, inc=1, device_id=(cut_peer(o), member), device_id_type=MESH)
    for o in range(1, 16):
        pl.semaphore_signal(barrier, inc=1, device_id=(cut, plane_peer(o)), device_id_type=MESH)

    load(0, 64, 192, 1)
    error_copy = pltpu.make_async_copy(errors, error_v, error_sem)
    error_copy.start()
    load(1, 0, 256, 2)

    for l in range(2):
        start[l] = (seed[l].astype(jnp.float32) - 32760.0) * (1.0 / 18918.0)

    data_send, data_recv = ((sa1, sb1), (sa2, sb2)), ((ra1, rb1), (ra2, rb2))
    scale_slot = ((0, 0), (0, 2), (0, 1), (0, 3), (1, 0), (1, 1))

    def data_copy(t, s, p, m):
        axis = ring[s if p == 0 else 1 - s]
        g, n = (0, m) if m < 2 else (1, m - 2)
        return pltpu.make_async_remote_copy(
            src_ref=data_send[p][g].at[t, s, n], dst_ref=data_recv[p][g].at[t, s, n],
            send_sem=send_sem.at[p, g], recv_sem=recv_sem.at[t, p, g, 0],
            device_id=axis["plus"] if m % 2 == 0 else axis["minus"], device_id_type=MESH)

    def scale_copy(t, s, p, g, side):
        axis = ring[s if p == 0 else 1 - s]
        rows = pl.ds(side * 2, 2) if g == 0 else pl.ds(side, 1)
        there, here = (rsa, ssa) if g == 0 else (rsb, ssb)
        return pltpu.make_async_remote_copy(
            src_ref=here.at[t, p, s, rows], dst_ref=there.at[t, p, s, rows],
            send_sem=send_sem.at[2, g], recv_sem=recv_sem.at[t, p, g, 1],
            device_id=axis["plus"] if side == 0 else axis["minus"], device_id_type=MESH)

    def arrived(t, p, g):
        there = data_recv[p][g].at[t]
        pltpu.make_async_copy(there, there, recv_sem.at[t, p, g, 0]).wait()
        there = (rsa, rsb)[g].at[t, p]
        pltpu.make_async_copy(there, there, recv_sem.at[t, p, g, 1]).wait()

    def rows_of(t, s, h):
        return pl.ds(pl.multiple_of(lax.rem(t, 4) * 64 + s * 32 + h * 16, 16), 16)

    def term(t, s, p, q, h):
        l, rows = lax.div(t, 4), rows_of(t, s, h)
        if p == 0:
            return own[l, :, q, :, rows, :] if s == 0 else own[l, q, :, :, rows, :]
        return own[l, q, y, :, rows, :] if s == 0 else own[l, z, q, :, rows, :]

    def code(t, s, p, m, values):
        coded, scale = quantize(values)
        g, n = (0, m) if m < 2 else (1, m - 2)
        data_send[p][g][t, s, n] = coded
        group, row = scale_slot[m]
        (ssa, ssb)[group][t, p, s, row] = scale

    def got(t, s, p, m):
        g, n = (0, m) if m < 2 else (1, m - 2)
        group, row = scale_slot[m]
        return restore(data_recv[p][g][t, s, n], (rsa, rsb)[group][t, p, s, row])

    def first_code(t, s, p):
        pos = ring[s if p == 0 else 1 - s]["pos"]
        code(t, s, p, 0, term(t, s, p, wrap(pos + 2), 0))
        code(t, s, p, 1, term(t, s, p, wrap(pos + 2), 1))
        code(t, s, p, 2, term(t, s, p, wrap(pos + 1), 1))
        code(t, s, p, 3, term(t, s, p, wrap(pos - 1), 0))

    def first_send(t, s, p):
        for side in range(2):
            scale_copy(t, s, p, 0, side).start()
        for m in range(4):
            data_copy(t, s, p, m).start()

    def second(t, s, p):
        pos = ring[s if p == 0 else 1 - s]["pos"]
        code(t, s, p, 4, term(t, s, p, wrap(pos + 1), 0) + got(t, s, p, 0))
        code(t, s, p, 5, term(t, s, p, wrap(pos - 1), 1) + got(t, s, p, 1))
        for side in range(2):
            scale_copy(t, s, p, 1, side).start()
            data_copy(t, s, p, 4 + side).start()

    def total(t, s, p, h):
        pos = ring[s if p == 0 else 1 - s]["pos"]
        pair = (3, 4) if h == 0 else (2, 5)
        return term(t, s, p, pos, h) + got(t, s, p, pair[0]) + got(t, s, p, pair[1])

    def left_copy(l, half, o):
        return pltpu.make_async_remote_copy(
            src_ref=left.at[l, half], dst_ref=left_all.at[l, half, o],
            send_sem=cut_send.at[0], recv_sem=cut_recv.at[l, half],
            device_id=(cut_peer(o), member), device_id_type=MESH)

    loaded(0, 0, 64, 0)
    for s in range(2):
        first_code(0, s, 0)
    pl.semaphore_wait(barrier, 22)

    def step(t, _):
        @pl.when(t < STEPS)
        def _():
            for s in range(2):
                first_send(t, s, 0)

        @pl.when((t >= 1) & (t < STEPS + 1))
        def _():
            arrived(t - 1, 0, 0)
            for s in range(2):
                second(t - 1, s, 0)

        @pl.when((t >= 2) & (t < STEPS + 2))
        def _():
            u = t - 2
            l = lax.div(u, 4)
            arrived(u, 0, 1)
            for s in range(2):
                for h in range(2):
                    summed = total(u, s, 0, h)
                    if s == 0:
                        own[l, :, y, :, rows_of(u, s, h), :] = summed
                    else:
                        own[l, z, :, :, rows_of(u, s, h), :] = summed
                first_code(u, s, 1)
                first_send(u, s, 1)

        @pl.when((t >= 3) & (t < STEPS + 3))
        def _():
            arrived(t - 3, 1, 0)
            for s in range(2):
                second(t - 3, s, 1)

        @pl.when(t >= 4)
        def _():
            u = t - 4
            l = lax.div(u, 4)
            arrived(u, 1, 1)

            @pl.when(u == 0)
            def _():
                error_copy.wait()

            for s in range(2):
                for h in range(2):
                    rows = rows_of(u, s, h)
                    summed = total(u, s, 1, h)
                    wide = jnp.concatenate([summed[i] for i in range(4)], axis=1)
                    merged[l, rows, :] = wide + error_v[l, rows, :]

            @pl.when(lax.rem(u, 2) == 1)
            def _():
                half = lax.div(lax.rem(u, 4), 2)
                rows = pl.ds(pl.multiple_of(half * 128, 128), 128)
                left[l, half] = lax.dot_general(
                    start[l], merged[l, rows, :], (((1,), (1,)), ((), ())),
                    precision=HIGHEST, preferred_element_type=jnp.float32)
                for o in range(1, 8):
                    left_copy(l, half, o).start()
                left_all[l, half, 0] = left[l, half]

        @pl.when(t + 1 < STEPS)
        def _():
            @pl.when(t + 1 == 1)
            def _():
                loaded(0, 64, 192, 1)

            @pl.when(t + 1 == 4)
            def _():
                loaded(1, 0, 256, 2)

            for s in range(2):
                first_code(t + 1, s, 0)

        return 0

    lax.fori_loop(0, STEPS + 4, step, 0)

    merged_copy = pltpu.make_async_copy(merged, merged_out, out_sem.at[0])
    merged_copy.start()

    def slot(c):
        return lax.rem(cut - c + 8, 8)

    vectors = []
    for l in range(2):
        halves = []
        for half in range(2):
            there = left_all.at[l, half, pl.ds(1, 7)]
            pltpu.make_async_copy(there, there, cut_recv.at[l, half]).wait()
            summed = left_all[l, half, slot(0)]
            for c in range(1, 8):
                summed = summed + left_all[l, half, slot(c)]
            halves.append(summed)
        vectors.append(jnp.concatenate(halves, axis=1))

    later = lax.broadcasted_iota(jnp.int32, (32, 1), 0)
    for k in range(32):
        for l in range(2):
            v = vectors[l][k:k + 1, :]
            size = jnp.sum(v * v, axis=1, keepdims=True) + 1e-6
            dots = jnp.sum(vectors[l] * v, axis=1, keepdims=True)
            basis[l, k:k + 1, :] = v / jnp.sqrt(size)
            vectors[l] = vectors[l] - jnp.where(later > k, dots / size, 0.0) * v

    for l in range(2):
        wide = jnp.dot(basis[l], merged[l], precision=HIGHEST, preferred_element_type=jnp.float32)
        for i in range(4):
            right[l * 4 + i] = wide[:, i * 128:(i + 1) * 128]
    rights = [pltpu.make_async_remote_copy(
        src_ref=right.at[cut_peer(o)], dst_ref=right_all.at[o],
        send_sem=cut_send.at[1], recv_sem=cut_recv.at[2, 0],
        device_id=(cut_peer(o), member), device_id_type=MESH) for o in range(1, 8)]
    for copy in rights:
        copy.start()
    right_all[0] = right[cut]

    def plane_copy(n, o, src, dst):
        return pltpu.make_async_remote_copy(
            src_ref=src, dst_ref=dst, send_sem=plane_send.at[n], recv_sem=plane_recv.at[n],
            device_id=(cut, plane_peer(o)), device_id_type=MESH)

    both = jnp.concatenate([basis[0], basis[1]] * 2, axis=0).T
    coded, scale = quantize(both)
    basis_send[0] = coded[:128]
    basis_send[1] = coded[128:]
    scale_send[0] = scale
    for o in range(1, 16):
        plane_copy(0, o, basis_send.at[core], basis_q.at[core, o]).start()
        plane_copy(1, o, scale_send.at[0], basis_s.at[o]).start()
    mine = [pltpu.make_async_copy(basis_send, basis_q.at[:, 0], out_sem.at[1]),
            pltpu.make_async_copy(scale_send.at[0], basis_s.at[0], out_sem.at[2])]
    for copy in mine:
        copy.start()

    def landed(there, sem):
        pltpu.make_async_copy(there, there, sem).wait()

    landed(right_all.at[pl.ds(1, 7)], cut_recv.at[2, 0])
    summed = right_all[slot(0)]
    for c in range(1, 8):
        summed = summed + right_all[slot(c)]
    right_full[0] = summed * 0.125
    for o in range(1, 8):
        pltpu.make_async_remote_copy(
            src_ref=right_full.at[0], dst_ref=right_full.at[o],
            send_sem=cut_send.at[2], recv_sem=cut_recv.at[2, 1],
            device_id=(cut_peer(o), member), device_id_type=MESH).start()
    landed(right_full.at[pl.ds(1, 7)], cut_recv.at[2, 1])

    for l in range(2):
        coded, scale = quantize(jnp.stack([right_full[slot(l * 4 + i)] for i in range(4)]))
        right_send[l] = coded
        scale_send[1 + l] = scale
    for o in range(1, 16):
        plane_copy(2, o, right_send.at[core], right_q.at[core, o]).start()
        plane_copy(3, o, scale_send.at[pl.ds(1, 2)], right_s.at[o]).start()
    more = [pltpu.make_async_copy(right_send, right_q.at[:, 0], out_sem.at[3]),
            pltpu.make_async_copy(scale_send.at[pl.ds(1, 2)], right_s.at[0], out_sem.at[4])]
    for copy in more:
        copy.start()

    def swap(n, ref):
        there = ref.at[core, pl.ds(1, 15)]
        return pltpu.make_async_remote_copy(
            src_ref=there, dst_ref=there, send_sem=swap_sem.at[0, n], recv_sem=swap_sem.at[1, n],
            device_id=(cut + 1 - 2 * core, member), device_id_type=MESH)

    landed(basis_q.at[core, pl.ds(1, 15)], plane_recv.at[0])
    swap(0, basis_q).start()
    landed(basis_s.at[pl.ds(1, 15)], plane_recv.at[1])
    landed(right_s.at[pl.ds(1, 15)], plane_recv.at[3])
    landed(right_q.at[core, pl.ds(1, 15)], plane_recv.at[2])
    swap(1, right_q).start()

    for p in range(2):
        for g in range(2):
            landed(data_send[p][g], send_sem.at[p, g])
    landed(ssa, send_sem.at[2, 0])
    landed(ssb, send_sem.at[2, 1])
    landed(left_all.at[:, :, pl.ds(1, 7)], cut_send.at[0])
    landed(right_all.at[pl.ds(1, 7)], cut_send.at[1])
    landed(right_full.at[pl.ds(1, 7)], cut_send.at[2])
    landed(basis_q.at[core, pl.ds(1, 15)], plane_send.at[0])
    landed(basis_s.at[pl.ds(1, 15)], plane_send.at[1])
    landed(right_q.at[core, pl.ds(1, 15)], plane_send.at[2])
    landed(right_s.at[pl.ds(1, 15)], plane_send.at[3])
    for copy in mine + more:
        copy.wait()
    merged_copy.wait()
    swap(0, basis_q).wait()
    swap(1, right_q).wait()


def decompress(member_ref, basis_q, basis_s, right_q, right_s, merged, gradient, new_error,
               bq, bs, rq, rs, mg, ne, out, scale_sem, load_sem, merged_sem, out_sem):
    scales = [pltpu.make_async_copy(basis_s, bs, scale_sem.at[0]),
              pltpu.make_async_copy(right_s, rs, scale_sem.at[1])]
    merges = pltpu.make_async_copy(merged, mg, merged_sem.at[0])
    loads = []
    for g in range(4):
        slots = pl.ds(4 * g, 4)
        loads.append([pltpu.make_async_copy(basis_q.at[:, slots], bq.at[:, slots], load_sem.at[g, 0]),
                      pltpu.make_async_copy(right_q.at[:, slots], rq.at[:, slots], load_sem.at[g, 1])])
    for copy in scales + loads[0] + loads[1] + loads[2] + loads[3] + [merges]:
        copy.start()
    for copy in scales:
        copy.wait()

    def split(values):
        high = values.astype(jnp.bfloat16)
        return high, (values - high.astype(jnp.float32)).astype(jnp.bfloat16)

    zero = jnp.zeros((32, 512), jnp.bfloat16)

    def approx_of(o):
        b = restore(jnp.concatenate([bq[0, o], bq[1, o]], axis=0), bs[o])
        lhs = jnp.concatenate(split(b), axis=1)
        result = []
        for l in range(2):
            r = restore(rq[l, o], rs[o, l])
            high, low = split(jnp.concatenate([r[i] for i in range(4)], axis=1))
            rows = [zero] * 8
            rows[l], rows[l + 2], rows[l + 4], rows[l + 6] = high, low, high, low
            result.append(jnp.dot(lhs, jnp.concatenate(rows, axis=0), preferred_element_type=jnp.float32))
        return result

    writes = []
    for o in range(16):
        if o % 4 == 0:
            for copy in loads[o // 4]:
                copy.wait()
        for l, approx in enumerate(approx_of(o)):
            out[o, l] = approx.astype(jnp.bfloat16)
        j = lax.rem(member_ref[0] - o + 16, 16)
        columns = pl.ds(pl.multiple_of(j * 512, 512), 512)
        writes.append(pltpu.make_async_copy(out.at[o], gradient.at[:, :, columns], out_sem.at[o]))
        writes[-1].start()
    merges.wait()
    for l, approx in enumerate(approx_of(0)):
        ne[l] = mg[l] - approx
    writes.append(pltpu.make_async_copy(ne, new_error, merged_sem.at[1]))
    writes[-1].start()
    for copy in writes:
        copy.wait()


def body(partials, errors, start_seed):
    f32, i16 = jnp.float32, jnp.int16
    vmem = pl.BlockSpec(memory_space=pltpu.VMEM)
    hbm = pl.BlockSpec(memory_space=pl.ANY)
    dma = pltpu.SemaphoreType.DMA
    limit = 60 * 1024 * 1024
    data = [pltpu.VMEM((STEPS, 2, n, *shape, 16, 128), i16) for shape in ((4, 4), (4,)) for n in (2, 4)]
    scales = [pltpu.VMEM((STEPS, 2, 2, n, 1, 128), f32) for n in (4, 2)]
    merged, basis_q, basis_s, right_q, right_s = pl.pallas_call(
        exchange,
        out_shape=(
            jax.ShapeDtypeStruct((2, 256, 512), f32),
            jax.ShapeDtypeStruct((2, 16, 128, 128), i16),
            jax.ShapeDtypeStruct((16, 1, 128), f32),
            jax.ShapeDtypeStruct((2, 16, 4, 32, 128), i16),
            jax.ShapeDtypeStruct((16, 2, 1, 128), f32),
        ),
        in_specs=[hbm, hbm, vmem],
        out_specs=(hbm,) * 5,
        scratch_shapes=[
            pltpu.VMEM((2, 4, 4, 4, 256, 128), f32),
            pltpu.VMEM((2, 256, 512), f32),
            pltpu.VMEM((2, 256, 512), f32),
            pltpu.VMEM((2, 32, 512), f32),
            *data, *data, *scales, *scales,
            pltpu.VMEM((2, 2, 32, 128), f32),
            pltpu.VMEM((2, 2, 8, 32, 128), f32),
            pltpu.VMEM((2, 32, 256), f32),
            pltpu.VMEM((8, 32, 128), f32),
            pltpu.VMEM((8, 32, 128), f32),
            pltpu.VMEM((8, 32, 128), f32),
            pltpu.VMEM((2, 128, 128), i16),
            pltpu.VMEM((2, 4, 32, 128), i16),
            pltpu.VMEM((3, 1, 128), f32),
            dma((3,)),
            dma,
            dma((5,)),
            dma((3, 2)),
            dma((STEPS, 2, 2, 2)),
            dma((3,)),
            dma((3, 2)),
            dma((4,)),
            dma((4,)),
            dma((2, 2)),
        ],
        compiler_params=pltpu.CompilerParams(
            collective_id=0, has_side_effects=True, vmem_limit_bytes=limit),
        name="exchange",
    )(partials.reshape(2, 256, 8192), errors.reshape(2, 256, 512), jnp.swapaxes(start_seed, 1, 2))

    member = lax.axis_index("intra").astype(jnp.int32).reshape(1)
    gradient, new_error = pl.pallas_call(
        decompress,
        out_shape=(
            jax.ShapeDtypeStruct((2, 256, 8192), jnp.bfloat16),
            jax.ShapeDtypeStruct((2, 256, 512), f32),
        ),
        in_specs=[pl.BlockSpec(memory_space=pltpu.SMEM)] + [hbm] * 5,
        out_specs=(hbm, hbm),
        scratch_shapes=[
            pltpu.VMEM((2, 16, 128, 128), i16),
            pltpu.VMEM((16, 1, 128), f32),
            pltpu.VMEM((2, 16, 4, 32, 128), i16),
            pltpu.VMEM((16, 2, 1, 128), f32),
            pltpu.VMEM((2, 256, 512), f32),
            pltpu.VMEM((2, 256, 512), f32),
            pltpu.VMEM((16, 2, 256, 512), jnp.bfloat16),
            dma((2,)),
            dma((4, 2)),
            dma((2,)),
            dma((16,)),
        ],
        compiler_params=pltpu.CompilerParams(vmem_limit_bytes=limit),
        name="decompress",
    )(member, basis_q, basis_s, right_q, right_s, merged)
    return gradient, new_error[None]


def solution(mesh):
    in_specs = (
        P("cuts", "intra", None, None, None),
        P("cuts", None, None, "intra"),
        P(None, "intra", None),
    )
    out_specs = (P(), P("cuts", None, None, "intra"))
    return jax.shard_map(body, mesh=mesh, in_specs=in_specs, out_specs=out_specs, check_vma=False)
```

```python
import functools

import jax
import jax.numpy as jnp
from jax import lax
from jax.experimental import pallas as pl
from jax.experimental.pallas import tpu as pltpu
from jax.sharding import PartitionSpec as P

MESH = pl.DeviceIdType.MESH
HIGHEST = lax.Precision.HIGHEST
STEPS = 8
LIMIT = 32767.0


def quantize(values):
    top = jnp.abs(values)
    while top.ndim > 2:
        top = jnp.max(top, axis=0)
    top = jnp.maximum(jnp.max(top, axis=0, keepdims=True), 1e-30)
    coded = jnp.round(values * (LIMIT / top)).astype(jnp.int32).astype(jnp.int16)
    return coded, top * (1.0 / LIMIT)


def restore(coded, scale):
    return coded.astype(jnp.int32).astype(jnp.float32) * scale


def exchange(part, errors, seed, merged_out, basis_q, right_q, factor_s,
             own, error_v, merged, mean, start,
             sa1, sb1, sa2, sb2, ra1, rb1, ra2, rb2, ssa, ssb, rsa, rsb,
             shares, left, left_all, vectors, basis, basis_send, right_send, scale_send,
             load_sem, error_sem, out_sem, send_sem, recv_sem, cut_send, cut_recv, left_recv,
             plane_send, plane_recv, swap_sem):
    cut = lax.axis_index("cuts")
    member = lax.axis_index("intra")
    y, z = lax.rem(member, 4), lax.div(member, 4)
    core = lax.rem(cut, 2)

    def wrap(v):
        return lax.rem(v + 8, 4)

    ring = (
        {"plus": (cut, z * 4 + wrap(y + 1)), "minus": (cut, z * 4 + wrap(y - 1)), "pos": y},
        {"plus": (cut, wrap(z + 1) * 4 + y), "minus": (cut, wrap(z - 1) * 4 + y), "pos": z},
    )

    def cut_peer(o):
        return lax.rem(cut + o, 8)

    def plane_peer(o):
        return lax.rem(member + o, 16)

    def load(l, first, count, sem):
        rows = pl.ds(first, count)

        def group(g, _):
            pltpu.make_async_copy(
                part.at[l, rows, pl.ds(pl.multiple_of(g * 128, 128), 128)],
                own.at[l, lax.div(g, 16), lax.rem(lax.div(g, 4), 4), lax.rem(g, 4), rows],
                load_sem.at[sem]).start()
            return 0

        lax.fori_loop(0, 64, group, 0)

    def loaded(l, first, count, sem):
        there = own.at[l, :, :, :, pl.ds(first, count)]
        pltpu.make_async_copy(there, there, load_sem.at[sem]).wait()

    load(0, 0, 64, 0)

    barrier = pltpu.get_barrier_semaphore()
    for o in range(1, 8):
        pl.semaphore_signal(barrier, inc=1, device_id=(cut_peer(o), member), device_id_type=MESH)
    for o in range(1, 16):
        pl.semaphore_signal(barrier, inc=1, device_id=(cut, plane_peer(o)), device_id_type=MESH)

    load(0, 64, 192, 1)
    error_copy = pltpu.make_async_copy(errors, error_v, error_sem)
    error_copy.start()
    load(1, 0, 256, 2)

    for l in range(2):
        start[l] = (seed[l].astype(jnp.float32) - 32760.0) * (1.0 / 18918.0)

    data_send, data_recv = ((sa1, sb1), (sa2, sb2)), ((ra1, rb1), (ra2, rb2))
    scale_slot = ((0, 0), (0, 2), (0, 1), (0, 3), (1, 0), (1, 1))

    def data_copy(t, s, p, m):
        axis = ring[s if p == 0 else 1 - s]
        g, n = (0, m) if m < 2 else (1, m - 2)
        return pltpu.make_async_remote_copy(
            src_ref=data_send[p][g].at[t, s, n], dst_ref=data_recv[p][g].at[t, s, n],
            send_sem=send_sem.at[p, g], recv_sem=recv_sem.at[t, p, g, 0],
            device_id=axis["plus"] if m % 2 == 0 else axis["minus"], device_id_type=MESH)

    def scale_copy(t, s, p, g, side):
        axis = ring[s if p == 0 else 1 - s]
        rows = pl.ds(side * 2, 2) if g == 0 else pl.ds(side, 1)
        there, here = (rsa, ssa) if g == 0 else (rsb, ssb)
        return pltpu.make_async_remote_copy(
            src_ref=here.at[t, p, s, rows], dst_ref=there.at[t, p, s, rows],
            send_sem=send_sem.at[2, g], recv_sem=recv_sem.at[t, p, g, 1],
            device_id=axis["plus"] if side == 0 else axis["minus"], device_id_type=MESH)

    def arrived(t, p, g):
        there = data_recv[p][g].at[t]
        pltpu.make_async_copy(there, there, recv_sem.at[t, p, g, 0]).wait()
        there = (rsa, rsb)[g].at[t, p]
        pltpu.make_async_copy(there, there, recv_sem.at[t, p, g, 1]).wait()

    def rows_of(t, s, h):
        return pl.ds(pl.multiple_of(lax.rem(t, 4) * 64 + s * 32 + h * 16, 16), 16)

    def term(t, s, p, q, h):
        l, rows = lax.div(t, 4), rows_of(t, s, h)
        if p == 0:
            return own[l, :, q, :, rows, :] if s == 0 else own[l, q, :, :, rows, :]
        return own[l, q, y, :, rows, :] if s == 0 else own[l, z, q, :, rows, :]

    def code(t, s, p, m, values):
        coded, scale = quantize(values)
        g, n = (0, m) if m < 2 else (1, m - 2)
        data_send[p][g][t, s, n] = coded
        group, row = scale_slot[m]
        (ssa, ssb)[group][t, p, s, row] = scale

    def got(t, s, p, m):
        g, n = (0, m) if m < 2 else (1, m - 2)
        group, row = scale_slot[m]
        return restore(data_recv[p][g][t, s, n], (rsa, rsb)[group][t, p, s, row])

    def first_code(t, s, p):
        pos = ring[s if p == 0 else 1 - s]["pos"]
        code(t, s, p, 0, term(t, s, p, wrap(pos + 2), 0))
        code(t, s, p, 1, term(t, s, p, wrap(pos + 2), 1))
        code(t, s, p, 2, term(t, s, p, wrap(pos + 1), 1))
        code(t, s, p, 3, term(t, s, p, wrap(pos - 1), 0))

    def first_send(t, s, p):
        for side in range(2):
            scale_copy(t, s, p, 0, side).start()
        for m in range(4):
            data_copy(t, s, p, m).start()

    def second(t, s, p):
        pos = ring[s if p == 0 else 1 - s]["pos"]
        code(t, s, p, 4, term(t, s, p, wrap(pos + 1), 0) + got(t, s, p, 0))
        code(t, s, p, 5, term(t, s, p, wrap(pos - 1), 1) + got(t, s, p, 1))
        for side in range(2):
            scale_copy(t, s, p, 1, side).start()
            data_copy(t, s, p, 4 + side).start()

    def total(t, s, p, h):
        pos = ring[s if p == 0 else 1 - s]["pos"]
        pair = (3, 4) if h == 0 else (2, 5)
        return term(t, s, p, pos, h) + got(t, s, p, pair[0]) + got(t, s, p, pair[1])

    def base_of(u):
        return lax.rem(u, 4) * 64

    def share_copy(u, o):
        rows = pl.ds(pl.multiple_of(base_of(u) + cut_peer(o) * 8, 8), 8)
        return pltpu.make_async_remote_copy(
            src_ref=merged.at[lax.div(u, 4), rows], dst_ref=shares.at[u, o],
            send_sem=cut_send.at[0], recv_sem=cut_recv.at[u, 0],
            device_id=(cut_peer(o), member), device_id_type=MESH)

    def mean_copy(u, o):
        rows = pl.ds(pl.multiple_of(base_of(u) + cut * 8, 8), 8)
        there = mean.at[lax.div(u, 4), rows]
        return pltpu.make_async_remote_copy(
            src_ref=there, dst_ref=there, send_sem=cut_send.at[1], recv_sem=cut_recv.at[u, 1],
            device_id=(cut_peer(o), member), device_id_type=MESH)

    def landed(there, sem):
        pltpu.make_async_copy(there, there, sem).wait()

    def slot(c):
        return lax.rem(cut - c + 8, 8)

    def plane_copy(l, n, o, src, dst):
        return pltpu.make_async_remote_copy(
            src_ref=src, dst_ref=dst, send_sem=plane_send.at[l, n], recv_sem=plane_recv.at[l, n],
            device_id=(cut, plane_peer(o)), device_id_type=MESH)

    def left_copy(l, half, o):
        return pltpu.make_async_remote_copy(
            src_ref=left.at[l, half], dst_ref=left_all.at[l, half, o],
            send_sem=cut_send.at[2], recv_sem=left_recv.at[l, half],
            device_id=(cut_peer(o), member), device_id_type=MESH)

    def own_factors(l):
        return (pltpu.make_async_copy(basis_send.at[l], basis_q.at[l, :, 0], out_sem.at[1, l]),
                pltpu.make_async_copy(right_send.at[l], right_q.at[l, :, 0], out_sem.at[2, l]),
                pltpu.make_async_copy(scale_send.at[l], factor_s.at[l, 0], out_sem.at[3, l]))

    gathered = (basis_q, right_q)

    def swap(l, n):
        there = gathered[n].at[l, core, pl.ds(1, 15)]
        return pltpu.make_async_remote_copy(
            src_ref=there, dst_ref=there, send_sem=swap_sem.at[0, l, n], recv_sem=swap_sem.at[1, l, n],
            device_id=(cut + 1 - 2 * core, member), device_id_type=MESH)

    def pass_on(l, n):
        landed(gathered[n].at[l, core, pl.ds(1, 15)], plane_recv.at[l, n])
        swap(l, n).start()

    def gather_left(l):
        for half in range(2):
            landed(left_all.at[l, half, pl.ds(1, 7)], left_recv.at[l, half])
            summed = left_all[l, half, slot(0)]
            for c in range(1, 8):
                summed = summed + left_all[l, half, slot(c)]
            vectors[:, half * 128:(half + 1) * 128] = summed

    def columns(g):
        later = lax.broadcasted_iota(jnp.int32, (32, 1), 0) - g * 8
        soon = lax.broadcasted_iota(jnp.int32, (8, 1), 0)
        block = vectors[...]
        rows = pl.ds(pl.multiple_of(g * 8, 8), 8)
        group = vectors[rows, :]
        done = []
        for i in range(8):
            v = group[i:i + 1, :]
            size = jnp.sum(v * v, axis=1, keepdims=True) + 1e-6
            done.append(v / jnp.sqrt(size))
            near = jnp.sum(group * v, axis=1, keepdims=True) / size
            group = group - jnp.where(soon > i, near, 0.0) * v
            dots = jnp.sum(block * v, axis=1, keepdims=True) / size
            block = block - jnp.where(later > i, dots, 0.0) * v
        vectors[...] = block
        basis[rows, :] = jnp.concatenate(done, axis=0)

    def send_basis(l):
        coded, scale = quantize(jnp.stack([basis[:, i * 128:(i + 1) * 128] for i in range(2)]))
        basis_send[l] = coded
        scale_send[l, 0] = scale
        for o in range(1, 16):
            plane_copy(l, 0, o, basis_send.at[l, core], basis_q.at[l, core, o]).start()

    def send_right(l):
        right = jnp.dot(basis[...], mean[l], precision=HIGHEST, preferred_element_type=jnp.float32) * 0.125
        coded, scale = quantize(jnp.stack([right[:, i * 128:(i + 1) * 128] for i in range(4)]))
        right_send[l, 0] = coded[:2]
        right_send[l, 1] = coded[2:]
        scale_send[l, 1] = scale
        for o in range(1, 16):
            plane_copy(l, 2, o, scale_send.at[l], factor_s.at[l, o]).start()
            plane_copy(l, 1, o, right_send.at[l, core], right_q.at[l, core, o]).start()
        for copy in own_factors(l):
            copy.start()

    loaded(0, 0, 64, 0)
    for s in range(2):
        first_code(0, s, 0)
    pl.semaphore_wait(barrier, 22)

    def step(t, _):
        @pl.when(t < STEPS)
        def _():
            for s in range(2):
                first_send(t, s, 0)

        @pl.when((t >= 1) & (t < STEPS + 1))
        def _():
            arrived(t - 1, 0, 0)
            for s in range(2):
                second(t - 1, s, 0)

        @pl.when((t >= 2) & (t < STEPS + 2))
        def _():
            u = t - 2
            l = lax.div(u, 4)
            arrived(u, 0, 1)
            for s in range(2):
                for h in range(2):
                    summed = total(u, s, 0, h)
                    if s == 0:
                        own[l, :, y, :, rows_of(u, s, h), :] = summed
                    else:
                        own[l, z, :, :, rows_of(u, s, h), :] = summed
                first_code(u, s, 1)
                first_send(u, s, 1)

        @pl.when((t >= 3) & (t < STEPS + 3))
        def _():
            arrived(t - 3, 1, 0)
            for s in range(2):
                second(t - 3, s, 1)

        @pl.when((t >= 4) & (t < STEPS + 4))
        def _():
            u = t - 4
            l = lax.div(u, 4)
            arrived(u, 1, 1)

            @pl.when(u == 0)
            def _():
                error_copy.wait()

            for s in range(2):
                for h in range(2):
                    rows = rows_of(u, s, h)
                    summed = total(u, s, 1, h)
                    wide = jnp.concatenate([summed[i] for i in range(4)], axis=1)
                    merged[l, rows, :] = wide + error_v[l, rows, :]

            for o in range(1, 8):
                share_copy(u, o).start()

            @pl.when(lax.rem(u, 2) == 1)
            def _():
                half = lax.div(lax.rem(u, 4), 2)
                rows = pl.ds(pl.multiple_of(half * 128, 128), 128)
                left[l, half] = lax.dot_general(
                    start[l], merged[l, rows, :], (((1,), (1,)), ((), ())),
                    precision=HIGHEST, preferred_element_type=jnp.float32)
                for o in range(1, 8):
                    left_copy(l, half, o).start()
                left_all[l, half, 0] = left[l, half]

        @pl.when((t >= 5) & (t < STEPS + 5))
        def _():
            u = t - 5
            l = lax.div(u, 4)
            landed(shares.at[u, pl.ds(1, 7)], cut_recv.at[u, 0])
            rows = pl.ds(pl.multiple_of(base_of(u) + cut * 8, 8), 8)
            shares[u, 0] = merged[l, rows, :]
            summed = shares[u, slot(0)]
            for c in range(1, 8):
                summed = summed + shares[u, slot(c)]
            mean[l, rows, :] = summed
            for o in range(1, 8):
                mean_copy(u, o).start()

        @pl.when(t >= 6)
        def _():
            u = t - 6
            landed(mean.at[lax.div(u, 4), pl.ds(pl.multiple_of(base_of(u), 64), 56)], cut_recv.at[u, 1])

        @pl.when(t == STEPS)
        def _():
            gather_left(0)

        @pl.when((t >= STEPS) & (t < STEPS + 4))
        def _():
            columns(t - STEPS)

        @pl.when(t == STEPS + 3)
        def _():
            send_basis(0)
            send_right(0)

        @pl.when(t == STEPS + 4)
        def _():
            gather_left(1)
            lax.fori_loop(0, 4, lambda g, _: (columns(g), 0)[1], 0)
            send_basis(1)

        @pl.when(t + 1 < STEPS)
        def _():
            @pl.when(t + 1 == 1)
            def _():
                loaded(0, 64, 192, 1)

            @pl.when(t + 1 == 4)
            def _():
                loaded(1, 0, 256, 2)

            for s in range(2):
                first_code(t + 1, s, 0)

        return 0

    lax.fori_loop(0, STEPS + 6, step, 0)

    merged_copy = pltpu.make_async_copy(merged, merged_out, out_sem.at[0, 0])
    merged_copy.start()
    send_right(1)
    for l, n in ((0, 0), (0, 1), (1, 0), (1, 1)):
        pass_on(l, n)

    for p in range(2):
        for g in range(2):
            landed(data_send[p][g], send_sem.at[p, g])
    landed(ssa, send_sem.at[2, 0])
    landed(ssb, send_sem.at[2, 1])
    for n in range(2):
        landed(shares.at[:, pl.ds(1, 7)], cut_send.at[n])
    landed(left_all.at[:, :, pl.ds(1, 7)], cut_send.at[2])
    for l in range(2):
        landed(factor_s.at[l, pl.ds(1, 15)], plane_recv.at[l, 2])
        for n in range(2):
            landed(gathered[n].at[l, core, pl.ds(1, 15)], plane_send.at[l, n])
        landed(factor_s.at[l, pl.ds(1, 15)], plane_send.at[l, 2])
        for copy in own_factors(l):
            copy.wait()
    merged_copy.wait()
    for l in range(2):
        for n in range(2):
            swap(l, n).wait()


def decompress(member_ref, basis_q, right_q, factor_s, merged, gradient, new_error,
               bq, rq, fs, mg, ne, out, scale_sem, load_sem, merged_sem, out_sem):
    scales = pltpu.make_async_copy(factor_s, fs, scale_sem)
    merges = pltpu.make_async_copy(merged, mg, merged_sem.at[0])
    loads = []
    for g in range(4):
        slots = pl.ds(4 * g, 4)
        loads.append(pltpu.make_async_copy(basis_q.at[:, :, slots], bq.at[:, :, slots], load_sem.at[g, 0]))
        loads.append(pltpu.make_async_copy(right_q.at[:, :, slots], rq.at[:, :, slots], load_sem.at[g, 1]))
    for copy in [scales] + loads + [merges]:
        copy.start()
    scales.wait()

    def split(values):
        high = values.astype(jnp.bfloat16)
        return high, (values - high.astype(jnp.float32)).astype(jnp.bfloat16)

    def approx_of(l, o):
        left, right = fs[l, o, 0], fs[l, o, 1]
        b = jnp.concatenate([restore(bq[l, i, o], left) for i in range(2)], axis=1)
        r = jnp.concatenate([restore(rq[l, i // 2, o, i % 2], right) for i in range(4)], axis=1)
        b_high, b_low = split(b)
        r_high, r_low = split(r)
        return lax.dot_general(
            jnp.concatenate([b_high, b_high, b_low], axis=0),
            jnp.concatenate([r_high, r_low, r_high], axis=0),
            (((0,), (0,)), ((), ())), preferred_element_type=jnp.float32)

    writes = []
    for o in range(16):
        if o % 4 == 0:
            loads[o // 2].wait()
            loads[o // 2 + 1].wait()
        for l in range(2):
            out[o, l] = approx_of(l, o).astype(jnp.bfloat16)
        j = lax.rem(member_ref[0] - o + 16, 16)
        columns = pl.ds(pl.multiple_of(j * 512, 512), 512)
        writes.append(pltpu.make_async_copy(out.at[o], gradient.at[:, :, columns], out_sem.at[o]))
        writes[-1].start()
    merges.wait()
    for l in range(2):
        ne[l] = mg[l] - approx_of(l, 0)
    writes.append(pltpu.make_async_copy(ne, new_error, merged_sem.at[1]))
    writes[-1].start()
    for copy in writes:
        copy.wait()


def body(partials, errors, start_seed):
    f32, i16 = jnp.float32, jnp.int16
    vmem = pl.BlockSpec(memory_space=pltpu.VMEM)
    hbm = pl.BlockSpec(memory_space=pl.ANY)
    dma = pltpu.SemaphoreType.DMA
    limit = 60 * 1024 * 1024
    data = [pltpu.VMEM((STEPS, 2, n, *shape, 16, 128), i16) for shape in ((4, 4), (4,)) for n in (2, 4)]
    scales = [pltpu.VMEM((STEPS, 2, 2, n, 1, 128), f32) for n in (4, 2)]
    merged, basis_q, right_q, factor_s = pl.pallas_call(
        exchange,
        out_shape=(
            jax.ShapeDtypeStruct((2, 256, 512), f32),
            jax.ShapeDtypeStruct((2, 2, 16, 32, 128), i16),
            jax.ShapeDtypeStruct((2, 2, 16, 2, 32, 128), i16),
            jax.ShapeDtypeStruct((2, 16, 2, 1, 128), f32),
        ),
        in_specs=[hbm, hbm, vmem],
        out_specs=(hbm,) * 4,
        scratch_shapes=[
            pltpu.VMEM((2, 4, 4, 4, 256, 128), f32),
            pltpu.VMEM((2, 256, 512), f32),
            pltpu.VMEM((2, 256, 512), f32),
            pltpu.VMEM((2, 256, 512), f32),
            pltpu.VMEM((2, 32, 512), f32),
            *data, *data, *scales, *scales,
            pltpu.VMEM((STEPS, 8, 8, 512), f32),
            pltpu.VMEM((2, 2, 32, 128), f32),
            pltpu.VMEM((2, 2, 8, 32, 128), f32),
            pltpu.VMEM((32, 256), f32),
            pltpu.VMEM((32, 256), f32),
            pltpu.VMEM((2, 2, 32, 128), i16),
            pltpu.VMEM((2, 2, 2, 32, 128), i16),
            pltpu.VMEM((2, 2, 1, 128), f32),
            dma((3,)),
            dma,
            dma((4, 2)),
            dma((3, 2)),
            dma((STEPS, 2, 2, 2)),
            dma((3,)),
            dma((STEPS, 2)),
            dma((2, 2)),
            dma((2, 3)),
            dma((2, 3)),
            dma((2, 2, 2)),
        ],
        compiler_params=pltpu.CompilerParams(
            collective_id=0, has_side_effects=True, vmem_limit_bytes=limit),
        name="exchange",
    )(partials.reshape(2, 256, 8192), errors.reshape(2, 256, 512), jnp.swapaxes(start_seed, 1, 2))

    member = lax.axis_index("intra").astype(jnp.int32).reshape(1)
    gradient, new_error = pl.pallas_call(
        decompress,
        out_shape=(
            jax.ShapeDtypeStruct((2, 256, 8192), jnp.bfloat16),
            jax.ShapeDtypeStruct((2, 256, 512), f32),
        ),
        in_specs=[pl.BlockSpec(memory_space=pltpu.SMEM)] + [hbm] * 4,
        out_specs=(hbm, hbm),
        scratch_shapes=[
            pltpu.VMEM((2, 2, 16, 32, 128), i16),
            pltpu.VMEM((2, 2, 16, 2, 32, 128), i16),
            pltpu.VMEM((2, 16, 2, 1, 128), f32),
            pltpu.VMEM((2, 256, 512), f32),
            pltpu.VMEM((2, 256, 512), f32),
            pltpu.VMEM((16, 2, 256, 512), jnp.bfloat16),
            dma,
            dma((4, 2)),
            dma((2,)),
            dma((16,)),
        ],
        compiler_params=pltpu.CompilerParams(vmem_limit_bytes=limit),
        name="decompress",
    )(member, basis_q, right_q, factor_s, merged)
    return gradient, new_error[None]


def solution(mesh):
    in_specs = (
        P("cuts", "intra", None, None, None),
        P("cuts", None, None, "intra"),
        P(None, "intra", None),
    )
    out_specs = (P(), P("cuts", None, None, "intra"))
    return jax.shard_map(body, mesh=mesh, in_specs=in_specs, out_specs=out_specs, check_vma=False)
```

```python
import functools

import jax
import jax.numpy as jnp
from jax import lax
from jax.experimental import pallas as pl
from jax.experimental.pallas import tpu as pltpu
from jax.sharding import PartitionSpec as P

MESH = pl.DeviceIdType.MESH
HIGHEST = lax.Precision.HIGHEST
STEPS = 8
LIMIT = 32767.0


def quantize(values):
    top = jnp.abs(values)
    while top.ndim > 2:
        top = jnp.max(top, axis=0)
    top = jnp.maximum(jnp.max(top, axis=0, keepdims=True), 1e-30)
    coded = jnp.round(values * (LIMIT / top)).astype(jnp.int32).astype(jnp.int16)
    return coded, top * (1.0 / LIMIT)


def restore(coded, scale):
    return coded.astype(jnp.int32).astype(jnp.float32) * scale


def exchange(part, errors, seed, merged_out, basis_q, right_q, factor_s,
             own, error_v, merged, mean, start,
             sa1, sb1, sa2, sb2, ra1, rb1, ra2, rb2, ssa, ssb, rsa, rsb,
             shares, left, left_all, vectors, basis, basis_send, right_send, scale_send,
             load_sem, error_sem, out_sem, send_sem, recv_sem, cut_send, cut_recv, left_recv,
             plane_send, plane_recv, swap_sem, ready):
    cut = lax.axis_index("cuts")
    member = lax.axis_index("intra")
    y, z = lax.rem(member, 4), lax.div(member, 4)
    core = lax.rem(cut, 2)

    def wrap(v):
        return lax.rem(v + 8, 4)

    ring = (
        {"plus": (cut, z * 4 + wrap(y + 1)), "minus": (cut, z * 4 + wrap(y - 1)), "pos": y},
        {"plus": (cut, wrap(z + 1) * 4 + y), "minus": (cut, wrap(z - 1) * 4 + y), "pos": z},
    )

    def cut_peer(o):
        return lax.rem(cut + o, 8)

    def plane_peer(o):
        return lax.rem(member + o, 16)

    def load(l, first, count, sem):
        rows = pl.ds(first, count)

        def group(g, _):
            pltpu.make_async_copy(
                part.at[l, rows, pl.ds(pl.multiple_of(g * 128, 128), 128)],
                own.at[l, lax.div(g, 16), lax.rem(lax.div(g, 4), 4), lax.rem(g, 4), rows],
                load_sem.at[sem]).start()
            return 0

        lax.fori_loop(0, 64, group, 0)

    def loaded(l, first, count, sem):
        there = own.at[l, :, :, :, pl.ds(first, count)]
        pltpu.make_async_copy(there, there, load_sem.at[sem]).wait()

    load(0, 0, 64, 0)

    barrier = pltpu.get_barrier_semaphore()
    x_side = [(cut_peer(2), member), (cut_peer(6), member), (cut + 1 - 2 * core, member)]
    for there in x_side + [ring[s][side] for s in range(2) for side in ("plus", "minus")]:
        pl.semaphore_signal(barrier, inc=1, device_id=there, device_id_type=MESH)

    load(0, 64, 192, 1)
    error_copy = pltpu.make_async_copy(errors, error_v, error_sem)
    error_copy.start()
    load(1, 0, 256, 2)

    for l in range(2):
        start[l] = (seed[l].astype(jnp.float32) - 32760.0) * (1.0 / 18918.0)

    data_send, data_recv = ((sa1, sb1), (sa2, sb2)), ((ra1, rb1), (ra2, rb2))
    scale_slot = ((0, 0), (0, 2), (0, 1), (0, 3), (1, 0), (1, 1))

    def data_copy(t, s, p, m):
        axis = ring[s if p == 0 else 1 - s]
        g, n = (0, m) if m < 2 else (1, m - 2)
        return pltpu.make_async_remote_copy(
            src_ref=data_send[p][g].at[t, s, n], dst_ref=data_recv[p][g].at[t, s, n],
            send_sem=send_sem.at[p, g], recv_sem=recv_sem.at[t, p, g, 0],
            device_id=axis["plus"] if m % 2 == 0 else axis["minus"], device_id_type=MESH)

    def scale_copy(t, s, p, g, side):
        axis = ring[s if p == 0 else 1 - s]
        rows = pl.ds(side * 2, 2) if g == 0 else pl.ds(side, 1)
        there, here = (rsa, ssa) if g == 0 else (rsb, ssb)
        return pltpu.make_async_remote_copy(
            src_ref=here.at[t, p, s, rows], dst_ref=there.at[t, p, s, rows],
            send_sem=send_sem.at[2, g], recv_sem=recv_sem.at[t, p, g, 1],
            device_id=axis["plus"] if side == 0 else axis["minus"], device_id_type=MESH)

    def arrived(t, p, g):
        there = data_recv[p][g].at[t]
        pltpu.make_async_copy(there, there, recv_sem.at[t, p, g, 0]).wait()
        there = (rsa, rsb)[g].at[t, p]
        pltpu.make_async_copy(there, there, recv_sem.at[t, p, g, 1]).wait()

    def rows_of(t, s, h):
        return pl.ds(pl.multiple_of(lax.rem(t, 4) * 64 + s * 32 + h * 16, 16), 16)

    def term(t, s, p, q, h):
        l, rows = lax.div(t, 4), rows_of(t, s, h)
        if p == 0:
            return own[l, :, q, :, rows, :] if s == 0 else own[l, q, :, :, rows, :]
        return own[l, q, y, :, rows, :] if s == 0 else own[l, z, q, :, rows, :]

    def code(t, s, p, m, values):
        coded, scale = quantize(values)
        g, n = (0, m) if m < 2 else (1, m - 2)
        data_send[p][g][t, s, n] = coded
        group, row = scale_slot[m]
        (ssa, ssb)[group][t, p, s, row] = scale

    def got(t, s, p, m):
        g, n = (0, m) if m < 2 else (1, m - 2)
        group, row = scale_slot[m]
        return restore(data_recv[p][g][t, s, n], (rsa, rsb)[group][t, p, s, row])

    def first_code(t, s, p):
        pos = ring[s if p == 0 else 1 - s]["pos"]
        code(t, s, p, 0, term(t, s, p, wrap(pos + 2), 0))
        code(t, s, p, 1, term(t, s, p, wrap(pos + 2), 1))
        code(t, s, p, 2, term(t, s, p, wrap(pos + 1), 1))
        code(t, s, p, 3, term(t, s, p, wrap(pos - 1), 0))

    def first_send(t, s, p):
        for side in range(2):
            scale_copy(t, s, p, 0, side).start()
        for m in range(4):
            data_copy(t, s, p, m).start()

    def second(t, s, p):
        pos = ring[s if p == 0 else 1 - s]["pos"]
        code(t, s, p, 4, term(t, s, p, wrap(pos + 1), 0) + got(t, s, p, 0))
        code(t, s, p, 5, term(t, s, p, wrap(pos - 1), 1) + got(t, s, p, 1))
        for side in range(2):
            scale_copy(t, s, p, 1, side).start()
            data_copy(t, s, p, 4 + side).start()

    def total(t, s, p, h):
        pos = ring[s if p == 0 else 1 - s]["pos"]
        pair = (3, 4) if h == 0 else (2, 5)
        return term(t, s, p, pos, h) + got(t, s, p, pair[0]) + got(t, s, p, pair[1])

    def base_of(u):
        return lax.rem(u, 4) * 64

    def share_copy(u, o):
        rows = pl.ds(pl.multiple_of(base_of(u) + cut_peer(o) * 8, 8), 8)
        return pltpu.make_async_remote_copy(
            src_ref=merged.at[lax.div(u, 4), rows], dst_ref=shares.at[u, o],
            send_sem=cut_send.at[0], recv_sem=cut_recv.at[u, 0],
            device_id=(cut_peer(o), member), device_id_type=MESH)

    def mean_copy(u, o):
        rows = pl.ds(pl.multiple_of(base_of(u) + cut * 8, 8), 8)
        there = mean.at[lax.div(u, 4), rows]
        return pltpu.make_async_remote_copy(
            src_ref=there, dst_ref=there, send_sem=cut_send.at[1], recv_sem=cut_recv.at[u, 1],
            device_id=(cut_peer(o), member), device_id_type=MESH)

    def landed(there, sem):
        pltpu.make_async_copy(there, there, sem).wait()

    def slot(c):
        return lax.rem(cut - c + 8, 8)

    def plane_copy(l, n, o, src, dst):
        return pltpu.make_async_remote_copy(
            src_ref=src, dst_ref=dst, send_sem=plane_send.at[l, n], recv_sem=plane_recv.at[l, n],
            device_id=(cut, plane_peer(o)), device_id_type=MESH)

    def left_copy(l, half, o):
        return pltpu.make_async_remote_copy(
            src_ref=left.at[l, half], dst_ref=left_all.at[l, half, o],
            send_sem=cut_send.at[2], recv_sem=left_recv.at[l, half],
            device_id=(cut_peer(o), member), device_id_type=MESH)

    def own_factors(l):
        return (pltpu.make_async_copy(basis_send.at[l], basis_q.at[l, :, 0], out_sem.at[1, l]),
                pltpu.make_async_copy(right_send.at[l], right_q.at[l, :, 0], out_sem.at[2, l]),
                pltpu.make_async_copy(scale_send.at[l], factor_s.at[l, 0], out_sem.at[3, l]))

    gathered = (basis_q, right_q)

    def swap(l, n):
        there = gathered[n].at[l, core, pl.ds(1, 15)]
        return pltpu.make_async_remote_copy(
            src_ref=there, dst_ref=there, send_sem=swap_sem.at[0, l, n], recv_sem=swap_sem.at[1, l, n],
            device_id=(cut + 1 - 2 * core, member), device_id_type=MESH)

    def pass_on(l, n):
        landed(gathered[n].at[l, core, pl.ds(1, 15)], plane_recv.at[l, n])
        swap(l, n).start()

    def gather_left(l):
        for half in range(2):
            landed(left_all.at[l, half, pl.ds(1, 7)], left_recv.at[l, half])
            summed = left_all[l, half, slot(0)]
            for c in range(1, 8):
                summed = summed + left_all[l, half, slot(c)]
            vectors[:, half * 128:(half + 1) * 128] = summed

    def columns(g):
        later = lax.broadcasted_iota(jnp.int32, (32, 1), 0) - g * 8
        soon = lax.broadcasted_iota(jnp.int32, (8, 1), 0)
        block = vectors[...]
        rows = pl.ds(pl.multiple_of(g * 8, 8), 8)
        group = vectors[rows, :]
        done = []
        for i in range(8):
            v = group[i:i + 1, :]
            size = jnp.sum(v * v, axis=1, keepdims=True) + 1e-6
            done.append(v / jnp.sqrt(size))
            near = jnp.sum(group * v, axis=1, keepdims=True) / size
            group = group - jnp.where(soon > i, near, 0.0) * v
            dots = jnp.sum(block * v, axis=1, keepdims=True) / size
            block = block - jnp.where(later > i, dots, 0.0) * v
        vectors[...] = block
        basis[rows, :] = jnp.concatenate(done, axis=0)

    def send_basis(l):
        coded, scale = quantize(jnp.stack([basis[:, i * 128:(i + 1) * 128] for i in range(2)]))
        basis_send[l] = coded
        scale_send[l, 0] = scale
        for o in range(1, 16):
            plane_copy(l, 0, o, basis_send.at[l, core], basis_q.at[l, core, o]).start()

    def send_right(l):
        right = jnp.dot(basis[...], mean[l], precision=HIGHEST, preferred_element_type=jnp.float32) * 0.125
        coded, scale = quantize(jnp.stack([right[:, i * 128:(i + 1) * 128] for i in range(4)]))
        right_send[l, 0] = coded[:2]
        right_send[l, 1] = coded[2:]
        scale_send[l, 1] = scale
        for o in range(1, 16):
            plane_copy(l, 2, o, scale_send.at[l], factor_s.at[l, o]).start()
            plane_copy(l, 1, o, right_send.at[l, core], right_q.at[l, core, o]).start()
        for copy in own_factors(l):
            copy.start()

    loaded(0, 0, 64, 0)
    for s in range(2):
        first_code(0, s, 0)
    pl.semaphore_wait(barrier, 7)

    def tell(n):
        for there in x_side:
            pl.semaphore_signal(ready.at[n], inc=1, device_id=there, device_id_type=MESH)

    tell(0)

    def step(t, _):
        @pl.when(t < STEPS)
        def _():
            for s in range(2):
                first_send(t, s, 0)

        @pl.when(t == 1)
        def _():
            pl.semaphore_wait(ready.at[0], 3)
            tell(1)

        @pl.when(t == 3)
        def _():
            pl.semaphore_wait(ready.at[1], 3)

        @pl.when((t >= 1) & (t < STEPS + 1))
        def _():
            arrived(t - 1, 0, 0)
            for s in range(2):
                second(t - 1, s, 0)

        @pl.when((t >= 2) & (t < STEPS + 2))
        def _():
            u = t - 2
            l = lax.div(u, 4)
            arrived(u, 0, 1)
            for s in range(2):
                for h in range(2):
                    summed = total(u, s, 0, h)
                    if s == 0:
                        own[l, :, y, :, rows_of(u, s, h), :] = summed
                    else:
                        own[l, z, :, :, rows_of(u, s, h), :] = summed
                first_code(u, s, 1)
                first_send(u, s, 1)

        @pl.when((t >= 3) & (t < STEPS + 3))
        def _():
            arrived(t - 3, 1, 0)
            for s in range(2):
                second(t - 3, s, 1)

        @pl.when((t >= 4) & (t < STEPS + 4))
        def _():
            u = t - 4
            l = lax.div(u, 4)
            arrived(u, 1, 1)

            @pl.when(u == 0)
            def _():
                error_copy.wait()

            for s in range(2):
                for h in range(2):
                    rows = rows_of(u, s, h)
                    summed = total(u, s, 1, h)
                    wide = jnp.concatenate([summed[i] for i in range(4)], axis=1)
                    merged[l, rows, :] = wide + error_v[l, rows, :]

            for o in range(1, 8):
                share_copy(u, o).start()

            @pl.when(lax.rem(u, 2) == 1)
            def _():
                half = lax.div(lax.rem(u, 4), 2)
                rows = pl.ds(pl.multiple_of(half * 128, 128), 128)
                left[l, half] = lax.dot_general(
                    start[l], merged[l, rows, :], (((1,), (1,)), ((), ())),
                    precision=HIGHEST, preferred_element_type=jnp.float32)
                for o in range(1, 8):
                    left_copy(l, half, o).start()
                left_all[l, half, 0] = left[l, half]

        @pl.when((t >= 5) & (t < STEPS + 5))
        def _():
            u = t - 5
            l = lax.div(u, 4)
            landed(shares.at[u, pl.ds(1, 7)], cut_recv.at[u, 0])
            rows = pl.ds(pl.multiple_of(base_of(u) + cut * 8, 8), 8)
            shares[u, 0] = merged[l, rows, :]
            summed = shares[u, slot(0)]
            for c in range(1, 8):
                summed = summed + shares[u, slot(c)]
            mean[l, rows, :] = summed
            for o in range(1, 8):
                mean_copy(u, o).start()

        @pl.when(t >= 6)
        def _():
            u = t - 6
            landed(mean.at[lax.div(u, 4), pl.ds(pl.multiple_of(base_of(u), 64), 56)], cut_recv.at[u, 1])

        @pl.when(t == STEPS)
        def _():
            gather_left(0)

        @pl.when((t >= STEPS) & (t < STEPS + 4))
        def _():
            columns(t - STEPS)

        @pl.when(t == STEPS + 3)
        def _():
            send_basis(0)
            send_right(0)

        @pl.when(t == STEPS + 4)
        def _():
            gather_left(1)
            lax.fori_loop(0, 4, lambda g, _: (columns(g), 0)[1], 0)
            send_basis(1)

        @pl.when(t + 1 < STEPS)
        def _():
            @pl.when(t + 1 == 1)
            def _():
                loaded(0, 64, 192, 1)

            @pl.when(t + 1 == 4)
            def _():
                loaded(1, 0, 256, 2)

            for s in range(2):
                first_code(t + 1, s, 0)

        return 0

    lax.fori_loop(0, STEPS + 6, step, 0)

    merged_copy = pltpu.make_async_copy(merged, merged_out, out_sem.at[0, 0])
    merged_copy.start()
    send_right(1)
    for l, n in ((0, 0), (0, 1), (1, 0), (1, 1)):
        pass_on(l, n)

    for p in range(2):
        for g in range(2):
            landed(data_send[p][g], send_sem.at[p, g])
    landed(ssa, send_sem.at[2, 0])
    landed(ssb, send_sem.at[2, 1])
    for n in range(2):
        landed(shares.at[:, pl.ds(1, 7)], cut_send.at[n])
    landed(left_all.at[:, :, pl.ds(1, 7)], cut_send.at[2])
    for l in range(2):
        landed(factor_s.at[l, pl.ds(1, 15)], plane_recv.at[l, 2])
        for n in range(2):
            landed(gathered[n].at[l, core, pl.ds(1, 15)], plane_send.at[l, n])
        landed(factor_s.at[l, pl.ds(1, 15)], plane_send.at[l, 2])
        for copy in own_factors(l):
            copy.wait()
    merged_copy.wait()
    for l in range(2):
        for n in range(2):
            swap(l, n).wait()


def decompress(member_ref, basis_q, right_q, factor_s, merged, gradient, new_error,
               bq, rq, fs, mg, ne, out, scale_sem, load_sem, merged_sem, out_sem):
    scales = pltpu.make_async_copy(factor_s, fs, scale_sem)
    merges = pltpu.make_async_copy(merged, mg, merged_sem.at[0])
    loads = []
    for g in range(4):
        slots = pl.ds(4 * g, 4)
        loads.append(pltpu.make_async_copy(basis_q.at[:, :, slots], bq.at[:, :, slots], load_sem.at[g, 0]))
        loads.append(pltpu.make_async_copy(right_q.at[:, :, slots], rq.at[:, :, slots], load_sem.at[g, 1]))
    for copy in [scales] + loads + [merges]:
        copy.start()
    scales.wait()

    def split(values):
        high = values.astype(jnp.bfloat16)
        return high, (values - high.astype(jnp.float32)).astype(jnp.bfloat16)

    def approx_of(l, o):
        left, right = fs[l, o, 0], fs[l, o, 1]
        b = jnp.concatenate([restore(bq[l, i, o], left) for i in range(2)], axis=1)
        r = jnp.concatenate([restore(rq[l, i // 2, o, i % 2], right) for i in range(4)], axis=1)
        b_high, b_low = split(b)
        r_high, r_low = split(r)
        return lax.dot_general(
            jnp.concatenate([b_high, b_high, b_low], axis=0),
            jnp.concatenate([r_high, r_low, r_high], axis=0),
            (((0,), (0,)), ((), ())), preferred_element_type=jnp.float32)

    writes = []
    for o in range(16):
        if o % 4 == 0:
            loads[o // 2].wait()
            loads[o // 2 + 1].wait()
        for l in range(2):
            out[o, l] = approx_of(l, o).astype(jnp.bfloat16)
        j = lax.rem(member_ref[0] - o + 16, 16)
        columns = pl.ds(pl.multiple_of(j * 512, 512), 512)
        writes.append(pltpu.make_async_copy(out.at[o], gradient.at[:, :, columns], out_sem.at[o]))
        writes[-1].start()
    merges.wait()
    for l in range(2):
        ne[l] = mg[l] - approx_of(l, 0)
    writes.append(pltpu.make_async_copy(ne, new_error, merged_sem.at[1]))
    writes[-1].start()
    for copy in writes:
        copy.wait()


def body(partials, errors, start_seed):
    f32, i16 = jnp.float32, jnp.int16
    vmem = pl.BlockSpec(memory_space=pltpu.VMEM)
    hbm = pl.BlockSpec(memory_space=pl.ANY)
    dma = pltpu.SemaphoreType.DMA
    limit = 60 * 1024 * 1024
    data = [pltpu.VMEM((STEPS, 2, n, *shape, 16, 128), i16) for shape in ((4, 4), (4,)) for n in (2, 4)]
    scales = [pltpu.VMEM((STEPS, 2, 2, n, 1, 128), f32) for n in (4, 2)]
    merged, basis_q, right_q, factor_s = pl.pallas_call(
        exchange,
        out_shape=(
            jax.ShapeDtypeStruct((2, 256, 512), f32),
            jax.ShapeDtypeStruct((2, 2, 16, 32, 128), i16),
            jax.ShapeDtypeStruct((2, 2, 16, 2, 32, 128), i16),
            jax.ShapeDtypeStruct((2, 16, 2, 1, 128), f32),
        ),
        in_specs=[hbm, hbm, vmem],
        out_specs=(hbm,) * 4,
        scratch_shapes=[
            pltpu.VMEM((2, 4, 4, 4, 256, 128), f32),
            pltpu.VMEM((2, 256, 512), f32),
            pltpu.VMEM((2, 256, 512), f32),
            pltpu.VMEM((2, 256, 512), f32),
            pltpu.VMEM((2, 32, 512), f32),
            *data, *data, *scales, *scales,
            pltpu.VMEM((STEPS, 8, 8, 512), f32),
            pltpu.VMEM((2, 2, 32, 128), f32),
            pltpu.VMEM((2, 2, 8, 32, 128), f32),
            pltpu.VMEM((32, 256), f32),
            pltpu.VMEM((32, 256), f32),
            pltpu.VMEM((2, 2, 32, 128), i16),
            pltpu.VMEM((2, 2, 2, 32, 128), i16),
            pltpu.VMEM((2, 2, 1, 128), f32),
            dma((3,)),
            dma,
            dma((4, 2)),
            dma((3, 2)),
            dma((STEPS, 2, 2, 2)),
            dma((3,)),
            dma((STEPS, 2)),
            dma((2, 2)),
            dma((2, 3)),
            dma((2, 3)),
            dma((2, 2, 2)),
            pltpu.SemaphoreType.REGULAR((2,)),
        ],
        compiler_params=pltpu.CompilerParams(
            collective_id=0, has_side_effects=True, vmem_limit_bytes=limit),
        name="exchange",
    )(partials.reshape(2, 256, 8192), errors.reshape(2, 256, 512), jnp.swapaxes(start_seed, 1, 2))

    member = lax.axis_index("intra").astype(jnp.int32).reshape(1)
    gradient, new_error = pl.pallas_call(
        decompress,
        out_shape=(
            jax.ShapeDtypeStruct((2, 256, 8192), jnp.bfloat16),
            jax.ShapeDtypeStruct((2, 256, 512), f32),
        ),
        in_specs=[pl.BlockSpec(memory_space=pltpu.SMEM)] + [hbm] * 4,
        out_specs=(hbm, hbm),
        scratch_shapes=[
            pltpu.VMEM((2, 2, 16, 32, 128), i16),
            pltpu.VMEM((2, 2, 16, 2, 32, 128), i16),
            pltpu.VMEM((2, 16, 2, 1, 128), f32),
            pltpu.VMEM((2, 256, 512), f32),
            pltpu.VMEM((2, 256, 512), f32),
            pltpu.VMEM((16, 2, 256, 512), jnp.bfloat16),
            dma,
            dma((4, 2)),
            dma((2,)),
            dma((16,)),
        ],
        compiler_params=pltpu.CompilerParams(vmem_limit_bytes=limit),
        name="decompress",
    )(member, basis_q, right_q, factor_s, merged)
    return gradient, new_error[None]


def solution(mesh):
    in_specs = (
        P("cuts", "intra", None, None, None),
        P("cuts", None, None, "intra"),
        P(None, "intra", None),
    )
    out_specs = (P(), P("cuts", None, None, "intra"))
    return jax.shard_map(body, mesh=mesh, in_specs=in_specs, out_specs=out_specs, check_vma=False)
```

```python
import functools

import jax
import jax.numpy as jnp
from jax import lax
from jax.experimental import pallas as pl
from jax.experimental.pallas import tpu as pltpu
from jax.sharding import PartitionSpec as P

MESH = pl.DeviceIdType.MESH
HIGHEST = lax.Precision.HIGHEST
STEPS = 8
LIMIT = 32767.0


def quantize(values):
    top = jnp.abs(values)
    while top.ndim > 2:
        top = jnp.max(top, axis=0)
    top = jnp.maximum(jnp.max(top, axis=0, keepdims=True), 1e-30)
    coded = jnp.round(values * (LIMIT / top)).astype(jnp.int32).astype(jnp.int16)
    return coded, top * (1.0 / LIMIT)


def restore(coded, scale):
    return coded.astype(jnp.int32).astype(jnp.float32) * scale


def exchange(part, errors, seed, merged_out, basis_q, right_q, factor_s,
             own, error_v, merged, mean, start,
             sa1, sb1, sa2, sb2, ra1, rb1, ra2, rb2, ssa, ssb, rsa, rsb,
             share_send, share_recv, mean_coded, share_scale, share_rscale, mean_scale, left, left_all, vectors, basis, basis_send, right_send, scale_send,
             load_sem, error_sem, out_sem, send_sem, recv_sem, cut_send, cut_recv, left_recv,
             plane_send, plane_recv, swap_sem, ready):
    cut = lax.axis_index("cuts")
    member = lax.axis_index("intra")
    y, z = lax.rem(member, 4), lax.div(member, 4)
    core = lax.rem(cut, 2)

    def wrap(v):
        return lax.rem(v + 8, 4)

    ring = (
        {"plus": (cut, z * 4 + wrap(y + 1)), "minus": (cut, z * 4 + wrap(y - 1)),
         "far": (cut, z * 4 + wrap(y + 2)), "pos": y},
        {"plus": (cut, wrap(z + 1) * 4 + y), "minus": (cut, wrap(z - 1) * 4 + y),
         "far": (cut, wrap(z + 2) * 4 + y), "pos": z},
    )

    def cut_peer(o):
        return lax.rem(cut + o, 8)

    def plane_peer(o):
        return lax.rem(member + o, 16)

    def load(l, first, count, sem):
        rows = pl.ds(first, count)

        def group(g, _):
            pltpu.make_async_copy(
                part.at[l, rows, pl.ds(pl.multiple_of(g * 128, 128), 128)],
                own.at[l, lax.div(g, 16), lax.rem(lax.div(g, 4), 4), lax.rem(g, 4), rows],
                load_sem.at[sem]).start()
            return 0

        lax.fori_loop(0, 64, group, 0)

    def loaded(l, first, count, sem):
        there = own.at[l, :, :, :, pl.ds(first, count)]
        pltpu.make_async_copy(there, there, load_sem.at[sem]).wait()

    load(0, 0, 64, 0)

    barrier = pltpu.get_barrier_semaphore()
    x_side = [(cut_peer(2), member), (cut_peer(6), member), (cut + 1 - 2 * core, member)]
    for there in x_side + [ring[s][side] for s in range(2) for side in ("plus", "minus")]:
        pl.semaphore_signal(barrier, inc=1, device_id=there, device_id_type=MESH)

    load(0, 64, 192, 1)
    error_copy = pltpu.make_async_copy(errors, error_v, error_sem)
    error_copy.start()
    load(1, 0, 256, 2)

    for l in range(2):
        start[l] = (seed[l].astype(jnp.float32) - 32760.0) * (1.0 / 18918.0)

    data_send, data_recv = ((sa1, sb1), (sa2, sb2)), ((ra1, rb1), (ra2, rb2))
    scale_slot = ((0, 0), (0, 2), (0, 1), (0, 3), (1, 0), (1, 1))

    def data_copy(t, s, p, m, direct=False):
        axis = ring[s if p == 0 else 1 - s]
        to = axis["far"] if direct and m < 2 else axis["plus"] if m % 2 == 0 else axis["minus"]
        g, n = (0, m) if m < 2 else (1, m - 2)
        return pltpu.make_async_remote_copy(
            src_ref=data_send[p][g].at[t, s, n], dst_ref=data_recv[p][g].at[t, s, n],
            send_sem=send_sem.at[p, g], recv_sem=recv_sem.at[t, p, g, 0],
            device_id=to, device_id_type=MESH)

    def scale_copy(t, s, p, g, side):
        axis = ring[s if p == 0 else 1 - s]
        rows = pl.ds(side * 2, 2) if g == 0 else pl.ds(side, 1)
        there, here = (rsa, ssa) if g == 0 else (rsb, ssb)
        return pltpu.make_async_remote_copy(
            src_ref=here.at[t, p, s, rows], dst_ref=there.at[t, p, s, rows],
            send_sem=send_sem.at[2, g], recv_sem=recv_sem.at[t, p, g, 1],
            device_id=axis["plus"] if side == 0 else axis["minus"], device_id_type=MESH)

    def direct_scale_copy(t, s, p, row):
        axis = ring[s if p == 0 else 1 - s]
        return pltpu.make_async_remote_copy(
            src_ref=ssa.at[t, p, s, pl.ds(row, 1)], dst_ref=rsa.at[t, p, s, pl.ds(row, 1)],
            send_sem=send_sem.at[2, 0], recv_sem=recv_sem.at[t, p, 0, 1],
            device_id=(axis["far"], axis["plus"], axis["far"], axis["minus"])[row], device_id_type=MESH)

    def arrived(t, p, g):
        there = data_recv[p][g].at[t]
        pltpu.make_async_copy(there, there, recv_sem.at[t, p, g, 0]).wait()
        there = (rsa, rsb)[g].at[t, p]
        pltpu.make_async_copy(there, there, recv_sem.at[t, p, g, 1]).wait()

    def div4(t):
        return t // 4 if isinstance(t, int) else lax.div(t, 4)

    def rem4(t):
        return t % 4 if isinstance(t, int) else lax.rem(t, 4)

    def at(first, size, unit):
        return pl.ds(first if isinstance(first, int) else pl.multiple_of(first, unit), size)

    def rows_of(t, s, h):
        return at(rem4(t) * 64 + s * 32 + h * 16, 16, 16)

    def term(t, s, p, q, h):
        l, rows = div4(t), rows_of(t, s, h)
        if p == 0:
            return own[l, :, q, :, rows, :] if s == 0 else own[l, q, :, :, rows, :]
        return own[l, q, y, :, rows, :] if s == 0 else own[l, z, q, :, rows, :]

    def code(t, s, p, m, values):
        coded, scale = quantize(values)
        g, n = (0, m) if m < 2 else (1, m - 2)
        data_send[p][g][t, s, n] = coded
        group, row = scale_slot[m]
        (ssa, ssb)[group][t, p, s, row] = scale

    def got(t, s, p, m):
        g, n = (0, m) if m < 2 else (1, m - 2)
        group, row = scale_slot[m]
        return restore(data_recv[p][g][t, s, n], (rsa, rsb)[group][t, p, s, row])

    def first_code(t, s, p):
        pos = ring[s if p == 0 else 1 - s]["pos"]
        code(t, s, p, 0, term(t, s, p, wrap(pos + 2), 0))
        code(t, s, p, 1, term(t, s, p, wrap(pos + 2), 1))
        code(t, s, p, 2, term(t, s, p, wrap(pos + 1), 1))
        code(t, s, p, 3, term(t, s, p, wrap(pos - 1), 0))

    def first_send(t, s, p):
        for side in range(2):
            scale_copy(t, s, p, 0, side).start()
        for m in range(4):
            data_copy(t, s, p, m).start()

    def direct_code(t, s, p):
        pos = ring[s if p == 0 else 1 - s]["pos"]
        first_code(t, s, p)
        code(t, s, p, 4, term(t, s, p, wrap(pos + 1), 0))
        code(t, s, p, 5, term(t, s, p, wrap(pos - 1), 1))

    def direct_send(t, s, p):
        for row in range(4):
            direct_scale_copy(t, s, p, row).start()
        for side in range(2):
            scale_copy(t, s, p, 1, side).start()
        for m in range(6):
            data_copy(t, s, p, m, True).start()

    def second(t, s, p):
        pos = ring[s if p == 0 else 1 - s]["pos"]
        code(t, s, p, 4, term(t, s, p, wrap(pos + 1), 0) + got(t, s, p, 0))
        code(t, s, p, 5, term(t, s, p, wrap(pos - 1), 1) + got(t, s, p, 1))
        for side in range(2):
            scale_copy(t, s, p, 1, side).start()
            data_copy(t, s, p, 4 + side).start()

    def total(t, s, p, h, direct=False):
        pos = ring[s if p == 0 else 1 - s]["pos"]
        pair = (3, 4) if h == 0 else (2, 5)
        summed = term(t, s, p, pos, h) + got(t, s, p, pair[0]) + got(t, s, p, pair[1])
        return summed + got(t, s, p, h) if direct else summed

    def base_of(u):
        return rem4(u) * 64

    def share_copies(u, o):
        return [pltpu.make_async_remote_copy(
            src_ref=src.at[u, cut_peer(o)], dst_ref=dst.at[u, o],
            send_sem=cut_send.at[n], recv_sem=cut_recv.at[u, n],
            device_id=(cut_peer(o), member), device_id_type=MESH)
            for n, (src, dst) in enumerate(((share_send, share_recv), (share_scale, share_rscale)))]

    def mean_copies(u, o):
        return [pltpu.make_async_remote_copy(
            src_ref=ref.at[u, cut], dst_ref=ref.at[u, cut],
            send_sem=cut_send.at[2 + n], recv_sem=cut_recv.at[u, 2 + n],
            device_id=(cut_peer(o), member), device_id_type=MESH)
            for n, ref in enumerate((mean_coded, mean_scale))]

    def fold(rows):
        slices = rows.reshape(8, 8, 512)
        columns = [slices[:, :, i * 128:(i + 1) * 128] for i in range(4)]
        pairs = [jnp.concatenate(columns[i:i + 2], axis=1) for i in (0, 2)]
        return jnp.stack(pairs, axis=1)

    def unfold(slices):
        columns = [slices[:, i // 2, (i % 2) * 8:(i % 2) * 8 + 8] for i in range(4)]
        return jnp.concatenate(columns, axis=2).reshape(64, 512)

    def landed(there, sem):
        pltpu.make_async_copy(there, there, sem).wait()

    def slot(c):
        return lax.rem(cut - c + 8, 8)

    def plane_copy(l, n, o, src, dst):
        return pltpu.make_async_remote_copy(
            src_ref=src, dst_ref=dst, send_sem=plane_send.at[l, n], recv_sem=plane_recv.at[l, n],
            device_id=(cut, plane_peer(o)), device_id_type=MESH)

    def left_copy(l, half, o):
        return pltpu.make_async_remote_copy(
            src_ref=left.at[l, half], dst_ref=left_all.at[l, half, o],
            send_sem=cut_send.at[4], recv_sem=left_recv.at[l, half],
            device_id=(cut_peer(o), member), device_id_type=MESH)

    def own_factors(l):
        return (pltpu.make_async_copy(basis_send.at[l], basis_q.at[l, :, 0], out_sem.at[1, l]),
                pltpu.make_async_copy(right_send.at[l], right_q.at[l, :, 0], out_sem.at[2, l]),
                pltpu.make_async_copy(scale_send.at[l], factor_s.at[l, 0], out_sem.at[3, l]))

    gathered = (basis_q, right_q)

    def swap(l, n):
        there = gathered[n].at[l, core, pl.ds(1, 15)]
        return pltpu.make_async_remote_copy(
            src_ref=there, dst_ref=there, send_sem=swap_sem.at[0, l, n], recv_sem=swap_sem.at[1, l, n],
            device_id=(cut + 1 - 2 * core, member), device_id_type=MESH)

    def pass_on(l, n):
        landed(gathered[n].at[l, core, pl.ds(1, 15)], plane_recv.at[l, n])
        swap(l, n).start()

    def gather_left(l):
        for half in range(2):
            landed(left_all.at[l, half, pl.ds(1, 7)], left_recv.at[l, half])
            summed = left_all[l, half, slot(0)]
            for c in range(1, 8):
                summed = summed + left_all[l, half, slot(c)]
            vectors[:, half * 128:(half + 1) * 128] = summed

    def columns(g):
        later = lax.broadcasted_iota(jnp.int32, (32, 1), 0) - g * 8
        soon = lax.broadcasted_iota(jnp.int32, (8, 1), 0)
        block = vectors[...]
        rows = at(g * 8, 8, 8)
        group = vectors[rows, :]
        done = []
        for i in range(8):
            v = group[i:i + 1, :]
            size = jnp.sum(v * v, axis=1, keepdims=True) + 1e-6
            done.append(v / jnp.sqrt(size))
            near = jnp.sum(group * v, axis=1, keepdims=True) / size
            group = group - jnp.where(soon > i, near, 0.0) * v
            dots = jnp.sum(block * v, axis=1, keepdims=True) / size
            block = block - jnp.where(later > i, dots, 0.0) * v
        vectors[...] = block
        basis[rows, :] = jnp.concatenate(done, axis=0)

    def send_basis(l):
        coded, scale = quantize(jnp.stack([basis[:, i * 128:(i + 1) * 128] for i in range(2)]))
        basis_send[l] = coded
        scale_send[l, 0] = scale
        for o in range(1, 16):
            plane_copy(l, 0, o, basis_send.at[l, core], basis_q.at[l, core, o]).start()

    def send_right(l):
        right = jnp.dot(basis[...], mean[l], precision=HIGHEST, preferred_element_type=jnp.float32) * 0.125
        coded, scale = quantize(jnp.stack([right[:, i * 128:(i + 1) * 128] for i in range(4)]))
        right_send[l, 0] = coded[:2]
        right_send[l, 1] = coded[2:]
        scale_send[l, 1] = scale
        for o in range(1, 16):
            plane_copy(l, 2, o, scale_send.at[l], factor_s.at[l, o]).start()
            plane_copy(l, 1, o, right_send.at[l, core], right_q.at[l, core, o]).start()
        for copy in own_factors(l):
            copy.start()

    loaded(0, 0, 64, 0)
    for s in range(2):
        first_code(0, s, 0)
    pl.semaphore_wait(barrier, 7)

    def tell(n):
        for there in x_side:
            pl.semaphore_signal(ready.at[n], inc=1, device_id=there, device_id_type=MESH)

    tell(0)

    def stage1(u):
        arrived(u, 0, 0)
        for s in range(2):
            second(u, s, 0)

    def stage2(u, direct=False, onward=False):
        l = div4(u)
        if direct:
            arrived(u, 0, 0)
        arrived(u, 0, 1)
        for s in range(2):
            for h in range(2):
                summed = total(u, s, 0, h, direct)
                if s == 0:
                    own[l, :, y, :, rows_of(u, s, h), :] = summed
                else:
                    own[l, z, :, :, rows_of(u, s, h), :] = summed
            (direct_code if onward else first_code)(u, s, 1)
            (direct_send if onward else first_send)(u, s, 1)

    def stage3(u):
        arrived(u, 1, 0)
        for s in range(2):
            second(u, s, 1)

    def stage4(u, direct=False):
        l = div4(u)
        if direct:
            arrived(u, 1, 0)
        arrived(u, 1, 1)
        for s in range(2):
            for h in range(2):
                rows = rows_of(u, s, h)
                summed = total(u, s, 1, h, direct)
                wide = jnp.concatenate([summed[i] for i in range(4)], axis=1)
                merged[l, rows, :] = wide + error_v[l, rows, :]
        folded = fold(merged[l, at(base_of(u), 64, 64), :])
        top = jnp.max(jnp.max(jnp.abs(folded), axis=1, keepdims=True), axis=2, keepdims=True)
        top = jnp.maximum(top, 1e-30)
        share_send[u] = jnp.round(folded * (LIMIT / top)).astype(jnp.int32).astype(jnp.int16)
        share_scale[u] = top[:, 0] * (1.0 / LIMIT)
        for o in range(1, 8):
            for copy in share_copies(u, o):
                copy.start()

    def send_left(l, half):
        left[l, half] = lax.dot_general(
            start[l], merged[l, pl.ds(half * 128, 128), :], (((1,), (1,)), ((), ())),
            precision=HIGHEST, preferred_element_type=jnp.float32)
        for o in range(1, 8):
            left_copy(l, half, o).start()
        left_all[l, half, 0] = left[l, half]

    def stage5(u):
        landed(share_recv.at[u, pl.ds(1, 7)], cut_recv.at[u, 0])
        landed(share_rscale.at[u, pl.ds(1, 7)], cut_recv.at[u, 1])
        summed = restore(share_send[u, cut], share_scale[u, cut])
        for o in range(1, 8):
            summed = summed + restore(share_recv[u, o], share_rscale[u, o])
        coded, scale = quantize(summed)
        mean_coded[u, cut] = coded
        mean_scale[u, cut] = scale
        for o in range(1, 8):
            for copy in mean_copies(u, o):
                copy.start()

    def stage6(u):
        landed(mean_coded.at[u, pl.ds(0, 7)], cut_recv.at[u, 2])
        landed(mean_scale.at[u, pl.ds(0, 7)], cut_recv.at[u, 3])
        mean[div4(u), at(base_of(u), 64, 64), :] = unfold(restore(mean_coded[u], mean_scale[u][:, None]))

    def step(t, _):
        for s in range(2):
            first_send(t, s, 0)

        @pl.when(t == 1)
        def _():
            pl.semaphore_wait(ready.at[0], 3)
            tell(1)

        @pl.when(t == 3)
        def _():
            pl.semaphore_wait(ready.at[1], 3)

        for lag, stage in ((1, stage1), (2, stage2), (3, stage3), (4, stage4)):
            @pl.when(t >= lag)
            def _():
                if lag == 4:
                    @pl.when(t == 4)
                    def _():
                        error_copy.wait()

                stage(t - lag)

        @pl.when(t + 1 < 6)
        def _():
            @pl.when(t + 1 == 1)
            def _():
                loaded(0, 64, 192, 1)

            @pl.when(t + 1 == 4)
            def _():
                loaded(1, 0, 256, 2)

            for s in range(2):
                first_code(t + 1, s, 0)

        return 0

    lax.fori_loop(0, 6, step, 0)
    stage5(0)
    for u in (6, 7):
        for s in range(2):
            (direct_code if u == 7 else first_code)(u, s, 0)
            (direct_send if u == 7 else first_send)(u, s, 0)
        stage1(u - 1)
        stage2(u - 2)
        stage3(u - 3)
        stage4(u - 4)
        send_left(0, u - 6)
        stage5(u - 5)
        stage6(u - 6)

    stage2(7, True, True)
    stage2(6, False, True)
    stage3(5)
    stage4(4)
    stage5(3)
    stage6(2)
    gather_left(0)
    columns(0)
    columns(1)

    stage4(7, True)
    stage4(6, True)
    stage4(5)
    send_left(1, 1)
    send_left(1, 0)
    stage5(4)
    stage6(3)
    columns(2)
    columns(3)
    send_basis(0)
    send_right(0)

    for u in (7, 6, 5):
        stage5(u)
    stage6(4)
    gather_left(1)
    lax.fori_loop(0, 4, lambda g, _: (columns(g), 0)[1], 0)
    send_basis(1)
    for u in (5, 6, 7):
        stage6(u)

    merged_copy = pltpu.make_async_copy(merged, merged_out, out_sem.at[0, 0])
    merged_copy.start()
    send_right(1)
    for l, n in ((0, 0), (0, 1), (1, 0), (1, 1)):
        pass_on(l, n)

    for p in range(2):
        for g in range(2):
            landed(data_send[p][g], send_sem.at[p, g])
    landed(ssa, send_sem.at[2, 0])
    landed(ssb, send_sem.at[2, 1])
    for n, ref in enumerate((share_recv, share_rscale, share_recv, share_rscale)):
        landed(ref.at[:, pl.ds(1, 7)], cut_send.at[n])
    landed(left_all.at[:, :, pl.ds(1, 7)], cut_send.at[4])
    for l in range(2):
        landed(factor_s.at[l, pl.ds(1, 15)], plane_recv.at[l, 2])
        for n in range(2):
            landed(gathered[n].at[l, core, pl.ds(1, 15)], plane_send.at[l, n])
        landed(factor_s.at[l, pl.ds(1, 15)], plane_send.at[l, 2])
        for copy in own_factors(l):
            copy.wait()
    merged_copy.wait()
    for l in range(2):
        for n in range(2):
            swap(l, n).wait()


def decompress(member_ref, basis_q, right_q, factor_s, merged, gradient, new_error,
               bq, rq, fs, mg, ne, out, scale_sem, load_sem, merged_sem, out_sem):
    scales = pltpu.make_async_copy(factor_s, fs, scale_sem)
    merges = pltpu.make_async_copy(merged, mg, merged_sem.at[0])
    loads = []
    for g in range(4):
        slots = pl.ds(4 * g, 4)
        loads.append(pltpu.make_async_copy(basis_q.at[:, :, slots], bq.at[:, :, slots], load_sem.at[g, 0]))
        loads.append(pltpu.make_async_copy(right_q.at[:, :, slots], rq.at[:, :, slots], load_sem.at[g, 1]))
    for copy in [scales] + loads + [merges]:
        copy.start()
    scales.wait()

    def split(values):
        high = values.astype(jnp.bfloat16)
        return high, (values - high.astype(jnp.float32)).astype(jnp.bfloat16)

    def approx_of(l, o):
        left, right = fs[l, o, 0], fs[l, o, 1]
        b = jnp.concatenate([restore(bq[l, i, o], left) for i in range(2)], axis=1)
        r = jnp.concatenate([restore(rq[l, i // 2, o, i % 2], right) for i in range(4)], axis=1)
        b_high, b_low = split(b)
        r_high, r_low = split(r)
        return lax.dot_general(
            jnp.concatenate([b_high, b_high, b_low], axis=0),
            jnp.concatenate([r_high, r_low, r_high], axis=0),
            (((0,), (0,)), ((), ())), preferred_element_type=jnp.float32)

    writes = []
    for o in range(16):
        if o % 4 == 0:
            loads[o // 2].wait()
            loads[o // 2 + 1].wait()
        for l in range(2):
            out[o, l] = approx_of(l, o).astype(jnp.bfloat16)
        j = lax.rem(member_ref[0] - o + 16, 16)
        columns = pl.ds(pl.multiple_of(j * 512, 512), 512)
        writes.append(pltpu.make_async_copy(out.at[o], gradient.at[:, :, columns], out_sem.at[o]))
        writes[-1].start()
    merges.wait()
    for l in range(2):
        ne[l] = mg[l] - approx_of(l, 0)
    writes.append(pltpu.make_async_copy(ne, new_error, merged_sem.at[1]))
    writes[-1].start()
    for copy in writes:
        copy.wait()


def body(partials, errors, start_seed):
    f32, i16 = jnp.float32, jnp.int16
    vmem = pl.BlockSpec(memory_space=pltpu.VMEM)
    hbm = pl.BlockSpec(memory_space=pl.ANY)
    dma = pltpu.SemaphoreType.DMA
    limit = 60 * 1024 * 1024
    data = [pltpu.VMEM((STEPS, 2, n, *shape, 16, 128), i16) for shape in ((4, 4), (4,)) for n in (2, 4)]
    scales = [pltpu.VMEM((STEPS, 2, 2, n, 1, 128), f32) for n in (4, 2)]
    merged, basis_q, right_q, factor_s = pl.pallas_call(
        exchange,
        out_shape=(
            jax.ShapeDtypeStruct((2, 256, 512), f32),
            jax.ShapeDtypeStruct((2, 2, 16, 32, 128), i16),
            jax.ShapeDtypeStruct((2, 2, 16, 2, 32, 128), i16),
            jax.ShapeDtypeStruct((2, 16, 2, 1, 128), f32),
        ),
        in_specs=[hbm, hbm, vmem],
        out_specs=(hbm,) * 4,
        scratch_shapes=[
            pltpu.VMEM((2, 4, 4, 4, 256, 128), f32),
            pltpu.VMEM((2, 256, 512), f32),
            pltpu.VMEM((2, 256, 512), f32),
            pltpu.VMEM((2, 256, 512), f32),
            pltpu.VMEM((2, 32, 512), f32),
            *data, *data, *scales, *scales,
            *[pltpu.VMEM((STEPS, 8, 2, 16, 128), i16)] * 3,
            *[pltpu.VMEM((STEPS, 8, 1, 128), f32)] * 3,
            pltpu.VMEM((2, 2, 32, 128), f32),
            pltpu.VMEM((2, 2, 8, 32, 128), f32),
            pltpu.VMEM((32, 256), f32),
            pltpu.VMEM((32, 256), f32),
            pltpu.VMEM((2, 2, 32, 128), i16),
            pltpu.VMEM((2, 2, 2, 32, 128), i16),
            pltpu.VMEM((2, 2, 1, 128), f32),
            dma((3,)),
            dma,
            dma((4, 2)),
            dma((3, 2)),
            dma((STEPS, 2, 2, 2)),
            dma((5,)),
            dma((STEPS, 4)),
            dma((2, 2)),
            dma((2, 3)),
            dma((2, 3)),
            dma((2, 2, 2)),
            pltpu.SemaphoreType.REGULAR((2,)),
        ],
        compiler_params=pltpu.CompilerParams(
            collective_id=0, has_side_effects=True, vmem_limit_bytes=limit),
        name="exchange",
    )(partials.reshape(2, 256, 8192), errors.reshape(2, 256, 512), jnp.swapaxes(start_seed, 1, 2))

    member = lax.axis_index("intra").astype(jnp.int32).reshape(1)
    gradient, new_error = pl.pallas_call(
        decompress,
        out_shape=(
            jax.ShapeDtypeStruct((2, 256, 8192), jnp.bfloat16),
            jax.ShapeDtypeStruct((2, 256, 512), f32),
        ),
        in_specs=[pl.BlockSpec(memory_space=pltpu.SMEM)] + [hbm] * 4,
        out_specs=(hbm, hbm),
        scratch_shapes=[
            pltpu.VMEM((2, 2, 16, 32, 128), i16),
            pltpu.VMEM((2, 2, 16, 2, 32, 128), i16),
            pltpu.VMEM((2, 16, 2, 1, 128), f32),
            pltpu.VMEM((2, 256, 512), f32),
            pltpu.VMEM((2, 256, 512), f32),
            pltpu.VMEM((16, 2, 256, 512), jnp.bfloat16),
            dma,
            dma((4, 2)),
            dma((2,)),
            dma((16,)),
        ],
        compiler_params=pltpu.CompilerParams(vmem_limit_bytes=limit),
        name="decompress",
    )(member, basis_q, right_q, factor_s, merged)
    return gradient, new_error[None]


def solution(mesh):
    in_specs = (
        P("cuts", "intra", None, None, None),
        P("cuts", None, None, "intra"),
        P(None, "intra", None),
    )
    out_specs = (P(), P("cuts", None, None, "intra"))
    return jax.shard_map(body, mesh=mesh, in_specs=in_specs, out_specs=out_specs, check_vma=False)
```

```python
import functools

import jax
import jax.numpy as jnp
from jax import lax
from jax.experimental import pallas as pl
from jax.experimental.pallas import tpu as pltpu
from jax.sharding import PartitionSpec as P

MESH = pl.DeviceIdType.MESH
HIGHEST = lax.Precision.HIGHEST
STEPS = 8
LIMIT = 32767.0


def quantize(values):
    top = jnp.abs(values)
    while top.ndim > 2:
        top = jnp.max(top, axis=0)
    top = jnp.maximum(jnp.max(top, axis=0, keepdims=True), 1e-30)
    coded = jnp.round(values * (LIMIT / top)).astype(jnp.int32).astype(jnp.int16)
    return coded, top * (1.0 / LIMIT)


def restore(coded, scale):
    return coded.astype(jnp.int32).astype(jnp.float32) * scale


def exchange(part, errors, seed, merged_out, basis_q, right_q, factor_s,
             own, error_v, merged, mean, start,
             sa1, sb1, sa2, sb2, ra1, rb1, ra2, rb2, ssa, ssb, rsa, rsb,
             share_send, share_recv, mean_coded, share_scale, share_rscale, mean_scale, left, left_all, vectors, basis, basis_send, right_send, scale_send,
             load_sem, error_sem, out_sem, send_sem, recv_sem, cut_send, cut_recv, left_recv,
             plane_send, plane_recv, swap_sem, ready, measure):
    cut = lax.axis_index("cuts")
    member = lax.axis_index("intra")
    y, z = lax.rem(member, 4), lax.div(member, 4)
    core = lax.rem(cut, 2)

    def wrap(v):
        return lax.rem(v + 8, 4)

    ring = (
        {"plus": (cut, z * 4 + wrap(y + 1)), "minus": (cut, z * 4 + wrap(y - 1)),
         "far": (cut, z * 4 + wrap(y + 2)), "pos": y},
        {"plus": (cut, wrap(z + 1) * 4 + y), "minus": (cut, wrap(z - 1) * 4 + y),
         "far": (cut, wrap(z + 2) * 4 + y), "pos": z},
    )

    def cut_peer(o):
        return lax.rem(cut + o, 8)

    def plane_peer(o):
        return lax.rem(member + o, 16)

    def load(l, first, count, sem):
        rows = pl.ds(first, count)

        def group(g, _):
            pltpu.make_async_copy(
                part.at[l, rows, pl.ds(pl.multiple_of(g * 128, 128), 128)],
                own.at[l, lax.div(g, 16), lax.rem(lax.div(g, 4), 4), lax.rem(g, 4), rows],
                load_sem.at[sem]).start()
            return 0

        lax.fori_loop(0, 64, group, 0)

    def loaded(l, first, count, sem):
        there = own.at[l, :, :, :, pl.ds(first, count)]
        pltpu.make_async_copy(there, there, load_sem.at[sem]).wait()

    load(0, 0, 64, 0)

    barrier = pltpu.get_barrier_semaphore()
    x_side = [(cut_peer(2), member), (cut_peer(6), member), (cut + 1 - 2 * core, member)]
    for there in x_side + [ring[s][side] for s in range(2) for side in ("plus", "minus")]:
        pl.semaphore_signal(barrier, inc=1, device_id=there, device_id_type=MESH)

    load(0, 64, 192, 1)
    error_copy = pltpu.make_async_copy(errors, error_v, error_sem)
    error_copy.start()
    load(1, 0, 256, 2)

    for l in range(2):
        start[l] = (seed[l].astype(jnp.float32) - 32760.0) * (1.0 / 18918.0)

    data_send, data_recv = ((sa1, sb1), (sa2, sb2)), ((ra1, rb1), (ra2, rb2))
    scale_slot = ((0, 0), (0, 2), (0, 1), (0, 3), (1, 0), (1, 1))

    def data_copy(t, s, p, m, direct=False):
        axis = ring[s if p == 0 else 1 - s]
        to = axis["far"] if direct and m < 2 else axis["plus"] if m % 2 == 0 else axis["minus"]
        g, n = (0, m) if m < 2 else (1, m - 2)
        return pltpu.make_async_remote_copy(
            src_ref=data_send[p][g].at[t, s, n], dst_ref=data_recv[p][g].at[t, s, n],
            send_sem=send_sem.at[p, g], recv_sem=recv_sem.at[t, p, g],
            device_id=to, device_id_type=MESH)

    def scale_copy(t, s, p, g, side):
        axis = ring[s if p == 0 else 1 - s]
        rows = pl.ds(side * 2, 2) if g == 0 else pl.ds(side, 1)
        there, here = (rsa, ssa) if g == 0 else (rsb, ssb)
        return pltpu.make_async_remote_copy(
            src_ref=here.at[t, p, s, rows], dst_ref=there.at[t, p, s, rows],
            send_sem=send_sem.at[2, g], recv_sem=recv_sem.at[t, p, g],
            device_id=axis["plus"] if side == 0 else axis["minus"], device_id_type=MESH)

    def direct_scale_copy(t, s, p, row):
        axis = ring[s if p == 0 else 1 - s]
        return pltpu.make_async_remote_copy(
            src_ref=ssa.at[t, p, s, pl.ds(row, 1)], dst_ref=rsa.at[t, p, s, pl.ds(row, 1)],
            send_sem=send_sem.at[2, 0], recv_sem=recv_sem.at[t, p, 0],
            device_id=(axis["far"], axis["plus"], axis["far"], axis["minus"])[row], device_id_type=MESH)

    def count(rows, sem):
        pltpu.make_async_copy(measure.at[pl.ds(0, rows)], measure.at[pl.ds(0, rows)], sem).wait()

    def arrived(t, p, g):
        count(((520, 1028), (136, 260))[p][g], recv_sem.at[t, p, g])

    def div4(t):
        return t // 4 if isinstance(t, int) else lax.div(t, 4)

    def rem4(t):
        return t % 4 if isinstance(t, int) else lax.rem(t, 4)

    def at(first, size, unit):
        return pl.ds(first if isinstance(first, int) else pl.multiple_of(first, unit), size)

    def rows_of(t, s, h):
        return at(rem4(t) * 64 + s * 32 + h * 16, 16, 16)

    def term(t, s, p, q, h):
        l, rows = div4(t), rows_of(t, s, h)
        if p == 0:
            return own[l, :, q, :, rows, :] if s == 0 else own[l, q, :, :, rows, :]
        return own[l, q, y, :, rows, :] if s == 0 else own[l, z, q, :, rows, :]

    def code(t, s, p, m, values):
        coded, scale = quantize(values)
        g, n = (0, m) if m < 2 else (1, m - 2)
        data_send[p][g][t, s, n] = coded
        group, row = scale_slot[m]
        (ssa, ssb)[group][t, p, s, row] = scale

    def got(t, s, p, m):
        g, n = (0, m) if m < 2 else (1, m - 2)
        group, row = scale_slot[m]
        return restore(data_recv[p][g][t, s, n], (rsa, rsb)[group][t, p, s, row])

    def first_code(t, s, p):
        pos = ring[s if p == 0 else 1 - s]["pos"]
        code(t, s, p, 0, term(t, s, p, wrap(pos + 2), 0))
        code(t, s, p, 1, term(t, s, p, wrap(pos + 2), 1))
        code(t, s, p, 2, term(t, s, p, wrap(pos + 1), 1))
        code(t, s, p, 3, term(t, s, p, wrap(pos - 1), 0))

    def first_send(t, s, p):
        for side in range(2):
            scale_copy(t, s, p, 0, side).start()
        for m in range(4):
            data_copy(t, s, p, m).start()

    def direct_code(t, s, p):
        pos = ring[s if p == 0 else 1 - s]["pos"]
        first_code(t, s, p)
        code(t, s, p, 4, term(t, s, p, wrap(pos + 1), 0))
        code(t, s, p, 5, term(t, s, p, wrap(pos - 1), 1))

    def direct_send(t, s, p):
        for row in range(4):
            direct_scale_copy(t, s, p, row).start()
        for side in range(2):
            scale_copy(t, s, p, 1, side).start()
        for m in range(6):
            data_copy(t, s, p, m, True).start()

    def second(t, s, p):
        pos = ring[s if p == 0 else 1 - s]["pos"]
        code(t, s, p, 4, term(t, s, p, wrap(pos + 1), 0) + got(t, s, p, 0))
        code(t, s, p, 5, term(t, s, p, wrap(pos - 1), 1) + got(t, s, p, 1))
        for side in range(2):
            scale_copy(t, s, p, 1, side).start()
            data_copy(t, s, p, 4 + side).start()

    def total(t, s, p, h, direct=False):
        pos = ring[s if p == 0 else 1 - s]["pos"]
        pair = (3, 4) if h == 0 else (2, 5)
        summed = term(t, s, p, pos, h) + got(t, s, p, pair[0]) + got(t, s, p, pair[1])
        return summed + got(t, s, p, h) if direct else summed

    def base_of(u):
        return rem4(u) * 64

    def share_copies(u, o):
        return [pltpu.make_async_remote_copy(
            src_ref=src.at[u, cut_peer(o)], dst_ref=dst.at[u, o],
            send_sem=cut_send.at[n], recv_sem=cut_recv.at[u, 0],
            device_id=(cut_peer(o), member), device_id_type=MESH)
            for n, (src, dst) in enumerate(((share_send, share_recv), (share_scale, share_rscale)))]

    def mean_copies(u, o):
        return [pltpu.make_async_remote_copy(
            src_ref=ref.at[u, cut], dst_ref=ref.at[u, cut],
            send_sem=cut_send.at[2 + n], recv_sem=cut_recv.at[u, 1],
            device_id=(cut_peer(o), member), device_id_type=MESH)
            for n, ref in enumerate((mean_coded, mean_scale))]

    def fold(rows):
        slices = rows.reshape(8, 8, 512)
        columns = [slices[:, :, i * 128:(i + 1) * 128] for i in range(4)]
        pairs = [jnp.concatenate(columns[i:i + 2], axis=1) for i in (0, 2)]
        return jnp.stack(pairs, axis=1)

    def unfold(slices):
        columns = [slices[:, i // 2, (i % 2) * 8:(i % 2) * 8 + 8] for i in range(4)]
        return jnp.concatenate(columns, axis=2).reshape(64, 512)

    def landed(there, sem):
        pltpu.make_async_copy(there, there, sem).wait()

    def slot(c):
        return lax.rem(cut - c + 8, 8)

    def plane_copy(l, n, o, src, dst):
        return pltpu.make_async_remote_copy(
            src_ref=src, dst_ref=dst, send_sem=plane_send.at[l, n], recv_sem=plane_recv.at[l, n],
            device_id=(cut, plane_peer(o)), device_id_type=MESH)

    def left_copy(l, half, o):
        return pltpu.make_async_remote_copy(
            src_ref=left.at[l, half], dst_ref=left_all.at[l, half, o],
            send_sem=cut_send.at[4], recv_sem=left_recv.at[l, half],
            device_id=(cut_peer(o), member), device_id_type=MESH)

    def own_factors(l):
        return (pltpu.make_async_copy(basis_send.at[l], basis_q.at[l, :, 0], out_sem.at[1, l]),
                pltpu.make_async_copy(right_send.at[l], right_q.at[l, :, 0], out_sem.at[2, l]),
                pltpu.make_async_copy(scale_send.at[l], factor_s.at[l, 0], out_sem.at[3, l]))

    gathered = (basis_q, right_q)

    def swap(l, n):
        there = gathered[n].at[l, core, pl.ds(1, 15)]
        return pltpu.make_async_remote_copy(
            src_ref=there, dst_ref=there, send_sem=swap_sem.at[0, l, n], recv_sem=swap_sem.at[1, l, n],
            device_id=(cut + 1 - 2 * core, member), device_id_type=MESH)

    def pass_on(l, n):
        landed(gathered[n].at[l, core, pl.ds(1, 15)], plane_recv.at[l, n])
        swap(l, n).start()

    def gather_left(l):
        for half in range(2):
            landed(left_all.at[l, half, pl.ds(1, 7)], left_recv.at[l, half])
            summed = left_all[l, half, slot(0)]
            for c in range(1, 8):
                summed = summed + left_all[l, half, slot(c)]
            vectors[:, half * 128:(half + 1) * 128] = summed

    def columns(g):
        later = lax.broadcasted_iota(jnp.int32, (32, 1), 0) - g * 8
        soon = lax.broadcasted_iota(jnp.int32, (8, 1), 0)
        block = vectors[...]
        rows = at(g * 8, 8, 8)
        group = vectors[rows, :]
        done = []
        for i in range(8):
            v = group[i:i + 1, :]
            size = jnp.sum(v * v, axis=1, keepdims=True) + 1e-6
            done.append(v / jnp.sqrt(size))
            near = jnp.sum(group * v, axis=1, keepdims=True) / size
            group = group - jnp.where(soon > i, near, 0.0) * v
            dots = jnp.sum(block * v, axis=1, keepdims=True) / size
            block = block - jnp.where(later > i, dots, 0.0) * v
        vectors[...] = block
        basis[rows, :] = jnp.concatenate(done, axis=0)

    def send_basis(l):
        coded, scale = quantize(jnp.stack([basis[:, i * 128:(i + 1) * 128] for i in range(2)]))
        basis_send[l] = coded
        scale_send[l, 0] = scale
        for o in range(1, 16):
            plane_copy(l, 0, o, basis_send.at[l, core], basis_q.at[l, core, o]).start()

    def send_right(l):
        right = jnp.dot(basis[...], mean[l], precision=HIGHEST, preferred_element_type=jnp.float32) * 0.125
        coded, scale = quantize(jnp.stack([right[:, i * 128:(i + 1) * 128] for i in range(4)]))
        right_send[l, 0] = coded[:2]
        right_send[l, 1] = coded[2:]
        scale_send[l, 1] = scale
        for o in range(1, 16):
            plane_copy(l, 2, o, scale_send.at[l], factor_s.at[l, o]).start()
            plane_copy(l, 1, o, right_send.at[l, core], right_q.at[l, core, o]).start()
        for copy in own_factors(l):
            copy.start()

    loaded(0, 0, 64, 0)
    for s in range(2):
        first_code(0, s, 0)
    pl.semaphore_wait(barrier, 7)

    def tell(n):
        for there in x_side:
            pl.semaphore_signal(ready.at[n], inc=1, device_id=there, device_id_type=MESH)

    tell(0)

    def stage1(u):
        arrived(u, 0, 0)
        for s in range(2):
            second(u, s, 0)

    def stage2(u, direct=False, onward=False):
        l = div4(u)
        if direct:
            arrived(u, 0, 0)
        arrived(u, 0, 1)
        for s in range(2):
            for h in range(2):
                summed = total(u, s, 0, h, direct)
                if s == 0:
                    own[l, :, y, :, rows_of(u, s, h), :] = summed
                else:
                    own[l, z, :, :, rows_of(u, s, h), :] = summed
            (direct_code if onward else first_code)(u, s, 1)
            (direct_send if onward else first_send)(u, s, 1)

    def stage3(u):
        arrived(u, 1, 0)
        for s in range(2):
            second(u, s, 1)

    def stage4(u, direct=False):
        l = div4(u)
        if direct:
            arrived(u, 1, 0)
        arrived(u, 1, 1)
        for s in range(2):
            for h in range(2):
                rows = rows_of(u, s, h)
                summed = total(u, s, 1, h, direct)
                wide = jnp.concatenate([summed[i] for i in range(4)], axis=1)
                merged[l, rows, :] = wide + error_v[l, rows, :]
        folded = fold(merged[l, at(base_of(u), 64, 64), :])
        top = jnp.max(jnp.max(jnp.abs(folded), axis=1, keepdims=True), axis=2, keepdims=True)
        top = jnp.maximum(top, 1e-30)
        share_send[u] = jnp.round(folded * (LIMIT / top)).astype(jnp.int32).astype(jnp.int16)
        share_scale[u] = top[:, 0] * (1.0 / LIMIT)
        for o in range(1, 8):
            for copy in share_copies(u, o):
                copy.start()

    def send_left(l, half):
        left[l, half] = lax.dot_general(
            start[l], merged[l, pl.ds(half * 128, 128), :], (((1,), (1,)), ((), ())),
            precision=HIGHEST, preferred_element_type=jnp.float32)
        for o in range(1, 8):
            left_copy(l, half, o).start()
        left_all[l, half, 0] = left[l, half]

    def stage5(u):
        count(119, cut_recv.at[u, 0])
        summed = restore(share_send[u, cut], share_scale[u, cut])
        for o in range(1, 8):
            summed = summed + restore(share_recv[u, o], share_rscale[u, o])
        coded, scale = quantize(summed)
        mean_coded[u, cut] = coded
        mean_scale[u, cut] = scale
        for o in range(1, 8):
            for copy in mean_copies(u, o):
                copy.start()

    def stage6(u):
        count(119, cut_recv.at[u, 1])
        mean[div4(u), at(base_of(u), 64, 64), :] = unfold(restore(mean_coded[u], mean_scale[u][:, None]))

    def step(t, _):
        for s in range(2):
            first_send(t, s, 0)

        @pl.when(t == 1)
        def _():
            pl.semaphore_wait(ready.at[0], 3)
            tell(1)

        @pl.when(t == 3)
        def _():
            pl.semaphore_wait(ready.at[1], 3)

        for lag, stage in ((1, stage1), (2, stage2), (3, stage3), (4, stage4)):
            @pl.when(t >= lag)
            def _():
                if lag == 4:
                    @pl.when(t == 4)
                    def _():
                        error_copy.wait()

                stage(t - lag)

        @pl.when(t + 1 < 6)
        def _():
            @pl.when(t + 1 == 1)
            def _():
                loaded(0, 64, 192, 1)

            @pl.when(t + 1 == 4)
            def _():
                loaded(1, 0, 256, 2)

            for s in range(2):
                first_code(t + 1, s, 0)

        return 0

    lax.fori_loop(0, 6, step, 0)
    stage5(0)
    for u in (6, 7):
        for s in range(2):
            (direct_code if u == 7 else first_code)(u, s, 0)
            (direct_send if u == 7 else first_send)(u, s, 0)
        stage1(u - 1)
        stage2(u - 2)
        stage3(u - 3)
        stage4(u - 4)
        send_left(0, u - 6)
        stage5(u - 5)
        stage6(u - 6)

    stage2(7, True, True)
    stage2(6, False, True)
    stage3(5)
    stage4(4)
    stage5(3)
    stage6(2)
    gather_left(0)
    columns(0)
    columns(1)

    stage4(7, True)
    stage4(6, True)
    stage4(5)
    send_left(1, 1)
    send_left(1, 0)
    stage5(4)
    stage6(3)
    columns(2)
    columns(3)
    send_basis(0)
    send_right(0)

    for u in (7, 6, 5):
        stage5(u)
    stage6(4)
    gather_left(1)
    lax.fori_loop(0, 4, lambda g, _: (columns(g), 0)[1], 0)
    send_basis(1)
    for u in (5, 6, 7):
        stage6(u)

    merged_copy = pltpu.make_async_copy(merged, merged_out, out_sem.at[0, 0])
    merged_copy.start()
    send_right(1)
    for l, n in ((0, 0), (0, 1), (1, 0), (1, 1)):
        pass_on(l, n)

    for p in range(2):
        for g in range(2):
            landed(data_send[p][g], send_sem.at[p, g])
    landed(ssa, send_sem.at[2, 0])
    landed(ssb, send_sem.at[2, 1])
    for n, ref in enumerate((share_recv, share_rscale, share_recv, share_rscale)):
        landed(ref.at[:, pl.ds(1, 7)], cut_send.at[n])
    landed(left_all.at[:, :, pl.ds(1, 7)], cut_send.at[4])
    for l in range(2):
        landed(factor_s.at[l, pl.ds(1, 15)], plane_recv.at[l, 2])
        for n in range(2):
            landed(gathered[n].at[l, core, pl.ds(1, 15)], plane_send.at[l, n])
        landed(factor_s.at[l, pl.ds(1, 15)], plane_send.at[l, 2])
        for copy in own_factors(l):
            copy.wait()
    merged_copy.wait()
    for l in range(2):
        for n in range(2):
            swap(l, n).wait()


def decompress(member_ref, basis_q, right_q, factor_s, merged, gradient, new_error,
               bq, rq, fs, mg, ne, out, scale_sem, load_sem, merged_sem, out_sem):
    scales = pltpu.make_async_copy(factor_s, fs, scale_sem)
    merges = pltpu.make_async_copy(merged, mg, merged_sem.at[0])
    loads = []
    for g in range(4):
        slots = pl.ds(4 * g, 4)
        loads.append(pltpu.make_async_copy(basis_q.at[:, :, slots], bq.at[:, :, slots], load_sem.at[g, 0]))
        loads.append(pltpu.make_async_copy(right_q.at[:, :, slots], rq.at[:, :, slots], load_sem.at[g, 1]))
    for copy in [scales] + loads + [merges]:
        copy.start()
    scales.wait()

    def split(values):
        high = values.astype(jnp.bfloat16)
        return high, (values - high.astype(jnp.float32)).astype(jnp.bfloat16)

    def approx_of(l, o):
        left, right = fs[l, o, 0], fs[l, o, 1]
        b = jnp.concatenate([restore(bq[l, i, o], left) for i in range(2)], axis=1)
        r = jnp.concatenate([restore(rq[l, i // 2, o, i % 2], right) for i in range(4)], axis=1)
        b_high, b_low = split(b)
        r_high, r_low = split(r)
        return lax.dot_general(
            jnp.concatenate([b_high, b_high, b_low], axis=0),
            jnp.concatenate([r_high, r_low, r_high], axis=0),
            (((0,), (0,)), ((), ())), preferred_element_type=jnp.float32)

    writes = []
    for o in range(16):
        if o % 4 == 0:
            loads[o // 2].wait()
            loads[o // 2 + 1].wait()
        for l in range(2):
            out[o, l] = approx_of(l, o).astype(jnp.bfloat16)
        j = lax.rem(member_ref[0] - o + 16, 16)
        columns = pl.ds(pl.multiple_of(j * 512, 512), 512)
        writes.append(pltpu.make_async_copy(out.at[o], gradient.at[:, :, columns], out_sem.at[o]))
        writes[-1].start()
    merges.wait()
    for l in range(2):
        ne[l] = mg[l] - approx_of(l, 0)
    writes.append(pltpu.make_async_copy(ne, new_error, merged_sem.at[1]))
    writes[-1].start()
    for copy in writes:
        copy.wait()


def body(partials, errors, start_seed):
    f32, i16 = jnp.float32, jnp.int16
    vmem = pl.BlockSpec(memory_space=pltpu.VMEM)
    hbm = pl.BlockSpec(memory_space=pl.ANY)
    dma = pltpu.SemaphoreType.DMA
    limit = 60 * 1024 * 1024
    data = [pltpu.VMEM((STEPS, 2, n, *shape, 16, 128), i16) for shape in ((4, 4), (4,)) for n in (2, 4)]
    scales = [pltpu.VMEM((STEPS, 2, 2, n, 1, 128), f32) for n in (4, 2)]
    merged, basis_q, right_q, factor_s = pl.pallas_call(
        exchange,
        out_shape=(
            jax.ShapeDtypeStruct((2, 256, 512), f32),
            jax.ShapeDtypeStruct((2, 2, 16, 32, 128), i16),
            jax.ShapeDtypeStruct((2, 2, 16, 2, 32, 128), i16),
            jax.ShapeDtypeStruct((2, 16, 2, 1, 128), f32),
        ),
        in_specs=[hbm, hbm, vmem],
        out_specs=(hbm,) * 4,
        scratch_shapes=[
            pltpu.VMEM((2, 4, 4, 4, 256, 128), f32),
            pltpu.VMEM((2, 256, 512), f32),
            pltpu.VMEM((2, 256, 512), f32),
            pltpu.VMEM((2, 256, 512), f32),
            pltpu.VMEM((2, 32, 512), f32),
            *data, *data, *scales, *scales,
            *[pltpu.VMEM((STEPS, 8, 2, 16, 128), i16)] * 3,
            *[pltpu.VMEM((STEPS, 8, 1, 128), f32)] * 3,
            pltpu.VMEM((2, 2, 32, 128), f32),
            pltpu.VMEM((2, 2, 8, 32, 128), f32),
            pltpu.VMEM((32, 256), f32),
            pltpu.VMEM((32, 256), f32),
            pltpu.VMEM((2, 2, 32, 128), i16),
            pltpu.VMEM((2, 2, 2, 32, 128), i16),
            pltpu.VMEM((2, 2, 1, 128), f32),
            dma((3,)),
            dma,
            dma((4, 2)),
            dma((3, 2)),
            dma((STEPS, 2, 2)),
            dma((5,)),
            dma((STEPS, 2)),
            dma((2, 2)),
            dma((2, 3)),
            dma((2, 3)),
            dma((2, 2, 2)),
            pltpu.SemaphoreType.REGULAR((2,)),
            pltpu.VMEM((1028, 1, 128), f32),
        ],
        compiler_params=pltpu.CompilerParams(
            collective_id=0, has_side_effects=True, vmem_limit_bytes=limit),
        name="exchange",
    )(partials.reshape(2, 256, 8192), errors.reshape(2, 256, 512), jnp.swapaxes(start_seed, 1, 2))

    member = lax.axis_index("intra").astype(jnp.int32).reshape(1)
    gradient, new_error = pl.pallas_call(
        decompress,
        out_shape=(
            jax.ShapeDtypeStruct((2, 256, 8192), jnp.bfloat16),
            jax.ShapeDtypeStruct((2, 256, 512), f32),
        ),
        in_specs=[pl.BlockSpec(memory_space=pltpu.SMEM)] + [hbm] * 4,
        out_specs=(hbm, hbm),
        scratch_shapes=[
            pltpu.VMEM((2, 2, 16, 32, 128), i16),
            pltpu.VMEM((2, 2, 16, 2, 32, 128), i16),
            pltpu.VMEM((2, 16, 2, 1, 128), f32),
            pltpu.VMEM((2, 256, 512), f32),
            pltpu.VMEM((2, 256, 512), f32),
            pltpu.VMEM((16, 2, 256, 512), jnp.bfloat16),
            dma,
            dma((4, 2)),
            dma((2,)),
            dma((16,)),
        ],
        compiler_params=pltpu.CompilerParams(vmem_limit_bytes=limit),
        name="decompress",
    )(member, basis_q, right_q, factor_s, merged)
    return gradient, new_error[None]


def solution(mesh):
    in_specs = (
        P("cuts", "intra", None, None, None),
        P("cuts", None, None, "intra"),
        P(None, "intra", None),
    )
    out_specs = (P(), P("cuts", None, None, "intra"))
    return jax.shard_map(body, mesh=mesh, in_specs=in_specs, out_specs=out_specs, check_vma=False)
```
